128 devices in a mesh: pair: 2 (over z_hi), row: 32 (over x, y, core), col: 2 (over z_lo).
Axes of the slice: x: 4, y: 4, z: 4 (z_hi: 2, z_lo: 2; z = z_hi * 2 + z_lo), core: 2. Of those that a mesh axis runs over, the one named last changes fastest.
Arguments:
- first_features: bfloat16 [256, 128, 128], P(('pair', 'row'), 'col'), parts along dimension 0, may hold values from -20 to 20
- second_features: bfloat16 [256, 128, 128], P(('pair', 'row'), 'col'), parts along dimension 0, may hold values from -20 to 20
- attend_weight: bfloat16 [128, 384], replicated, may hold values from -0.5 to 0.5
- merge_weight: bfloat16 [128, 128], replicated, may hold values from -0.5 to 0.5
- message_gain: float32 [128], replicated, may hold values from 0.3 to 1.7
- message_bias: float32 [128], replicated, may hold values from -3 to 3
- expand_weight: bfloat16 [256, 1024], replicated, may hold values from -0.375 to 0.375
- reduce_weight: bfloat16 [1024, 128], replicated, may hold values from -0.1875 to 0.1875
- update_gain: float32 [128], replicated, may hold values from 0.5 to 1.5
- update_bias: float32 [128], replicated, may hold values from -3 to 3
Outputs:
- flow_field: float32 [2, 256, 128], P(None, ('pair', 'row'), 'col'), parts along dimension 1
The draws below stay inside these ranges and needn't reach their ends.
There are 2 independent parts, one for each index of `pair`. The reference program is written for one: setup_inputs(seed, part) draws one part's arguments, and reference() takes and returns one part's arrays. A program takes and returns all parts, laid end to end along the dimension named above; an argument that names none is the same for every part. Nothing has to cross between parts.
All inputs are finite; a program needn't handle non-finite values.
Results may differ from the reference program's by a relative error of at most 0.019.
Values may be sent and summed in bfloat16 or wider, within the bound.
A program may use at most 64 MiB of HBM per device.

```python
import math
import jax
import jax.numpy as jnp
from jax import lax

CHAN = 128
HEADS = 8
HIDDEN_FF = 1024
HEAD_DIM = 16
ROWS = 128
COLS = 128
WIN_ROWS = 64
WIN_COLS = 64


def feature_field(key):
    subkeys = jax.random.split(jax.random.fold_in(key, 11), 2)
    base_field = jax.random.normal(subkeys[0], (ROWS, COLS, CHAN), jnp.float32)
    cell_scale = jnp.exp(jax.random.uniform(subkeys[1], (ROWS, COLS, 1), jnp.float32, -0.4, 0.4))
    feature = base_field * cell_scale
    return jnp.clip(feature, -20.0, 20.0)


def draw_first_features(key, part):
    return feature_field(key).astype(jnp.bfloat16)


def draw_second_features(key, part):
    feature = feature_field(key)
    subkeys = jax.random.split(jax.random.fold_in(key, 29), 3)
    row_step = jax.random.randint(subkeys[0], (ROWS, COLS), -(ROWS // 4), ROWS // 4 + 1)
    column_step = jax.random.randint(subkeys[1], (ROWS, COLS), -(COLS // 4), COLS // 4 + 1)
    source_row = (jnp.arange(ROWS, dtype=jnp.int32)[:, None] + row_step) % ROWS
    source_column = (jnp.arange(COLS, dtype=jnp.int32)[None, :] + column_step) % COLS
    shifted = feature[source_row, source_column]
    jitter = 0.5 * jax.random.normal(subkeys[2], (ROWS, COLS, CHAN), jnp.float32)
    return jnp.clip(shifted + jitter, -20.0, 20.0).astype(jnp.bfloat16)


def scatter_about(rng, shape, deviation, bound, kind=jnp.bfloat16):
    entries = jax.random.normal(rng, shape, jnp.float32) * deviation
    return jnp.minimum(jnp.maximum(entries, -bound), bound).astype(kind)


def setup_inputs(seed: int = 0, part: int = 0) -> dict:
    key_of = jax.random.split(jax.random.key(seed), 11)
    own_keys = jax.random.split(jax.random.fold_in(key_of[10], part), 11)
    first_features = draw_first_features(jax.random.fold_in(jax.random.fold_in(key_of[10], part), 71), part)
    second_features = draw_second_features(jax.random.fold_in(jax.random.fold_in(key_of[10], part), 71), part)
    attend_weight = scatter_about(key_of[2], (CHAN, 3 * CHAN), CHAN ** -0.5, 0.5)
    merge_weight = scatter_about(key_of[3], (CHAN, CHAN), CHAN ** -0.5, 0.5)
    message_gain = jnp.clip(jax.random.uniform(key_of[4], (CHAN,), jnp.float32, 0.3, 1.7), 0.3, 1.7)
    message_bias = scatter_about(key_of[5], (CHAN,), 0.5, 3.0, jnp.float32)
    expand_weight = scatter_about(key_of[6], (2 * CHAN, HIDDEN_FF), (2 * CHAN) ** -0.5, 0.375)
    reduce_weight = scatter_about(key_of[7], (HIDDEN_FF, CHAN), HIDDEN_FF ** -0.5, 0.1875)
    update_gain = jnp.clip(1.0 + 0.1 * jax.random.normal(key_of[8], (CHAN,), jnp.float32), 0.5, 1.5)
    update_bias = scatter_about(key_of[9], (CHAN,), 0.5, 3.0, jnp.float32)
    return {"first_features": first_features, "second_features": second_features, "attend_weight": attend_weight, "merge_weight": merge_weight, "message_gain": message_gain, "message_bias": message_bias, "expand_weight": expand_weight, "reduce_weight": reduce_weight, "update_gain": update_gain, "update_bias": update_bias}


NORM_EPSILON = 1e-05
MASKED = -1e+30

def layer_norm(values, scale_by, shift_by):
    centre = values - lax.optimization_barrier(jnp.mean(values, axis=-1, keepdims=True))
    spread = lax.optimization_barrier(jnp.mean(centre * centre, axis=-1, keepdims=True))
    return centre * lax.rsqrt(spread + NORM_EPSILON) * scale_by + shift_by

def window_attention(window, allowed):
    length = window.shape[0]
    queries = window[:, :CHAN].reshape(length, HEADS, HEAD_DIM).astype(jnp.float32).transpose(1, 0, 2)
    key_part = window[:, CHAN:2 * CHAN].reshape(length, HEADS, HEAD_DIM).astype(jnp.float32).transpose(1, 0, 2)
    value_part = window[:, 2 * CHAN:].reshape(length, HEADS, HEAD_DIM).astype(jnp.float32).transpose(1, 0, 2)
    head_scale = 1.0 / math.sqrt(HEAD_DIM)

    def one_head(operands):
        head_query, head_key, head_value = operands
        scores = jnp.dot(head_query, head_key.T) * head_scale
        scores = jnp.where(allowed[None, :], scores, MASKED)
        row_max = lax.optimization_barrier(jnp.max(scores, axis=1, keepdims=True))
        lifted = jnp.where(allowed[None, :], jnp.exp(scores - row_max), 0.0)
        total = lax.optimization_barrier(jnp.sum(lifted, axis=1, keepdims=True))
        soft = lax.optimization_barrier(lifted.astype(jnp.bfloat16)).astype(jnp.float32)
        return jnp.dot(soft, head_value) / total
    outputs = lax.map(one_head, (queries, key_part, value_part))
    return outputs.transpose(1, 0, 2).reshape(length, CHAN).astype(jnp.bfloat16)

def refine_frame(frame_in, attend_weight, merge_weight, message_gain, message_bias, expand_weight, reduce_weight, update_gain, update_bias):
    projected = jnp.dot(frame_in.reshape(ROWS * COLS, CHAN), attend_weight, preferred_element_type=jnp.float32)
    projected = projected.astype(jnp.bfloat16).reshape(ROWS, COLS, 3 * CHAN)
    row_margin = WIN_ROWS // 2
    column_margin = WIN_COLS // 2
    padded = jnp.pad(projected, ((row_margin, row_margin), (column_margin, column_margin), (0, 0)))
    inside = jnp.pad(jnp.ones((ROWS, COLS), jnp.int32), ((row_margin, row_margin), (column_margin, column_margin))) == 1
    tile_rows = (ROWS + 2 * row_margin) // WIN_ROWS
    tile_columns = (COLS + 2 * column_margin) // WIN_COLS
    windows = padded.reshape(tile_rows, WIN_ROWS, tile_columns, WIN_COLS, 3 * CHAN).transpose(0, 2, 1, 3, 4)
    windows = windows.reshape(tile_rows * tile_columns, WIN_ROWS * WIN_COLS, 3 * CHAN)
    allowed = inside.reshape(tile_rows, WIN_ROWS, tile_columns, WIN_COLS).transpose(0, 2, 1, 3)
    allowed = allowed.reshape(tile_rows * tile_columns, WIN_ROWS * WIN_COLS)
    attended = lax.map(lambda operands: window_attention(operands[0], operands[1]), (windows, allowed))
    attended = attended.reshape(tile_rows, tile_columns, WIN_ROWS, WIN_COLS, CHAN).transpose(0, 2, 1, 3, 4)
    attended = attended.reshape(tile_rows * WIN_ROWS, tile_columns * WIN_COLS, CHAN)
    attended = attended[row_margin:row_margin + ROWS, column_margin:column_margin + COLS].reshape(ROWS * COLS, CHAN)
    source = frame_in.reshape(ROWS * COLS, CHAN)
    message = layer_norm(jnp.dot(attended, merge_weight, preferred_element_type=jnp.float32), message_gain, message_bias).astype(jnp.bfloat16)
    joined = jnp.concatenate([source, message], axis=1)
    hidden = jax.nn.gelu(jnp.dot(joined, expand_weight, preferred_element_type=jnp.float32), approximate=False).astype(jnp.bfloat16)
    update = layer_norm(jnp.dot(hidden, reduce_weight, preferred_element_type=jnp.float32), update_gain, update_bias)
    return (source.astype(jnp.float32) + update).astype(jnp.bfloat16)

def reference(first_features, second_features, attend_weight, merge_weight, message_gain, message_bias, expand_weight, reduce_weight, update_gain, update_bias):
    weight_set = (attend_weight, merge_weight, message_gain, message_bias, expand_weight, reduce_weight, update_gain, update_bias)
    refined_one = refine_frame(first_features, *weight_set)
    refined_two = refine_frame(second_features, *weight_set)
    cell_ids = jnp.arange(ROWS * COLS, dtype=jnp.int32)
    source_column = (cell_ids % COLS).astype(jnp.float32)
    source_row = (cell_ids // COLS).astype(jnp.float32)
    score_scale = 1.0 / math.sqrt(CHAN)

    def expect(queries):
        scores = jnp.dot(queries, refined_two.T, preferred_element_type=jnp.float32) * score_scale
        row_max = lax.optimization_barrier(jnp.max(scores, axis=1, keepdims=True))
        lifted = jnp.exp(scores - row_max)
        run_sum = lax.optimization_barrier(jnp.sum(lifted, axis=1))
        along_column = lax.optimization_barrier(jnp.sum(lifted * source_column[None, :], axis=1)) / run_sum
        along_row = lax.optimization_barrier(jnp.sum(lifted * source_row[None, :], axis=1)) / run_sum
        return jnp.stack([along_column, along_row])
    blocks = refined_one.reshape(ROWS, COLS, CHAN)
    expected = lax.map(expect, blocks)
    expected = expected.transpose(1, 0, 2).reshape(2, ROWS, COLS)
    flow_column = (expected[0] - source_column.reshape(ROWS, COLS)) * (2.0 / COLS)
    flow_row = (expected[1] - source_row.reshape(ROWS, COLS)) * (2.0 / ROWS)
    return jnp.stack([flow_column, flow_row])
```

```python
import functools
import math

import jax
import jax.numpy as jnp
from jax import lax
from jax.experimental import pallas as pl
from jax.experimental.pallas import tpu as pltpu
from jax.sharding import PartitionSpec as P

HEADS = 8
HEAD_DIM = 16
CHAN = 128
HIDDEN = 1024
NORM_EPSILON = 1e-05
LOG2E = math.log2(math.e)
MESH = pl.DeviceIdType.MESH
F32 = jnp.float32
BF16 = jnp.bfloat16

HALF = 128
TILE = 256
CHUNK = 1024
CORNER, EDGE, OWN, OTHER = 8, 16, 8, 24
UNITS = 18
GROUP = 8


def nn(a, b):
    return jnp.dot(a, b, preferred_element_type=F32)


def nt(a, b):
    return lax.dot_general(a, b, (((1,), (1,)), ((), ())), preferred_element_type=F32)


def layer_norm(values, gain, bias):
    centre = values - jnp.mean(values, axis=-1, keepdims=True)
    spread = jnp.mean(centre * centre, axis=-1, keepdims=True)
    return centre * lax.rsqrt(spread + NORM_EPSILON) * gain + bias


def erf_gelu(x):
    return 0.5 * x * (1.0 + lax.erf(x * (1.0 / math.sqrt(2.0))))


def unit_tile(n):
    tile = jnp.where(n < 4, n, jnp.where(n < 20, 4 + (n - 4) // 2, 12 + (n - 20) // 4))
    chunk = jnp.where(n < 4, 0, jnp.where(n < 20, 1 + lax.rem(n, 2), 3 + lax.rem(n, 4)))
    return tile, chunk


def kernel(
    first, second, attend_w, merge_w, message_gain, message_bias, expand_w, reduce_w, update_gain, update_bias,
    out,
    sent, corner, edge, own, other,
    q_all, k_all, v_all, scores_a, scores_b, max_a, max_b, accs, maxes,
    o_all, attended, ref_q, ref_k, where_v, partial, parts,
    send_sem, corner_sem, edge_sem, own_sem, other_sem,
    back_send_sem, back_sem, ref_send_sem, q_sem, k_sem, part_send_sem, part_sem,
):
    pair, r, c = lax.axis_index("pair"), lax.axis_index("row"), lax.axis_index("col")
    me = r * 2 + c
    side = r // 16
    place = lax.rem(r, 16)
    head, frame = place // 2, lax.rem(place, 2)
    middle = (r >= 8) & (r < 24)

    barrier = pltpu.get_barrier_semaphore()

    def greet(i, carry):
        peer = lax.rem(me + 1 + i, 64)
        pl.semaphore_signal(barrier, inc=1, device_id=(pair, peer // 2, lax.rem(peer, 2)), device_id_type=MESH)
        return carry

    lax.fori_loop(0, 63, greet, 0)

    weight_t = attend_w[...].T
    for f, source in enumerate((first, second)):
        for half in range(2):
            cells = source[:, 32 * half : 32 * half + 32, :].reshape(HALF, CHAN)
            projected = nt(weight_t, cells)
            queries = projected[:CHAN] * (LOG2E / math.sqrt(HEAD_DIM))
            sent[f, half, :, 0:16, :] = queries.astype(BF16).reshape(HEADS, 16, HALF)
            sent[f, half, :, 16:32, :] = projected[CHAN : 2 * CHAN].astype(BF16).reshape(HEADS, 16, HALF)
            sent[f, half, :, 32:48, :] = projected[2 * CHAN :].astype(BF16).reshape(HEADS, 16, HALF)

    pl.semaphore_wait(barrier, 63)

    def transfer(source, target, dest_r, dest_c, s_sem, r_sem, start):
        here = (dest_r == r) & (dest_c == c)

        @pl.when(jnp.logical_not(here))
        def _():
            copy = pltpu.make_async_remote_copy(
                source, target, s_sem, r_sem, device_id=(pair, dest_r, dest_c), device_id_type=MESH
            )
            if start:
                copy.start()
            else:
                copy.wait_send()

        if start:

            @pl.when(here)
            def _():
                pltpu.make_async_copy(source, target, r_sem).start()

    def send_all(start):
        def each(body):
            def step(i, carry):
                d = lax.rem(place + i, 16)
                body(d // 2, lax.rem(d, 2), d)
                return carry

            lax.fori_loop(0, 16, step, 0)

        inner = 1 - c

        @pl.when(middle)
        def _():
            def outer_half(h, f, d):
                transfer(sent.at[f, c, h], edge.at[r - 8], (1 - c) * 16 + d, c, send_sem, edge_sem, start)

            def own_half(h, f, d):
                transfer(sent.at[f, inner, h], own.at[lax.rem(r, 8)], side * 16 + d, c, send_sem, own_sem, start)

            def other_halves(h, f, d):
                for turn in range(1, 4):
                    to_side, to_c = side ^ (turn // 2), c ^ (turn % 2)
                    transfer(
                        sent.at[f, inner, h, 16:48],
                        other.at[(turn - 1) * 8 + lax.rem(r, 8)],
                        to_side * 16 + d, to_c, send_sem, other_sem, start,
                    )

            each(outer_half)
            each(own_half)
            each(other_halves)

        @pl.when(jnp.logical_not(middle))
        def _():
            def corner_half(h, f, d):
                transfer(sent.at[f, c, h], corner.at[lax.rem(r, 8)], side * 16 + d, c, send_sem, corner_sem, start)

            def edge_half(h, f, d):
                slot = c * 8 + lax.rem(r, 8)
                transfer(sent.at[f, inner, h], edge.at[slot], side * 16 + d, side, send_sem, edge_sem, start)

            each(corner_half)
            each(edge_half)

    send_all(True)

    def arrived(ref, sem):
        pltpu.make_async_copy(ref, ref, sem).wait()

    def take_kv(block, at, first_row):
        k_all[at * HALF : (at + 1) * HALF, :] = block[first_row : first_row + 16, :].astype(F32).T.astype(BF16)
        v_all[0:16, at * HALF : (at + 1) * HALF] = block[first_row + 16 : first_row + 32, :]

    def take_q(block, at):
        q_all[at // 2, :, (at % 2) * HALF : (at % 2 + 1) * HALF] = block[0:16, :]

    v_all[16:32, :] = jnp.ones_like(v_all[16:32, :])
    arrived(corner, corner_sem)
    for b in range(CORNER):
        take_kv(corner[b], b, 16)
        take_q(corner[b], b)
    arrived(edge, edge_sem)
    for b in range(EDGE):
        take_kv(edge[b], 8 + b, 16)
        take_q(edge[b], 8 + b)

    def score_pass(u, scores, top):
        for sub in range(2):
            tile, chunk = unit_tile(2 * u + sub)
            keys = k_all[pl.ds(pl.multiple_of(chunk * CHUNK, CHUNK), CHUNK), :]
            x = nn(keys, q_all[tile])
            scores[sub * CHUNK : (sub + 1) * CHUNK, :] = x
            top[sub] = jnp.max(x.reshape(CHUNK // 8, 8, TILE), axis=0)

    def value_pass(u, scores, top):
        for sub in range(2):
            n = 2 * u + sub
            _, chunk = unit_tile(n)
            values = v_all[:, pl.ds(pl.multiple_of(chunk * CHUNK, CHUNK), CHUNK)]
            m = jnp.max(top[sub], axis=0, keepdims=True)
            p = jnp.exp2(scores[sub * CHUNK : (sub + 1) * CHUNK, :] - m).astype(BF16)
            accs[n] = nn(values, p)
            maxes[n] = jnp.broadcast_to(m, (8, TILE))

    def finish(tile, n, count):
        m = maxes[n, 0:1]
        for j in range(1, count):
            m = jnp.maximum(m, maxes[n + j, 0:1])
        acc = accs[n] * jnp.exp2(maxes[n, 0:1] - m)
        for j in range(1, count):
            acc = acc + accs[n + j] * jnp.exp2(maxes[n + j, 0:1] - m)
        o = (acc[0:16] / acc[16:17]).astype(BF16)
        o_all[2 * tile] = o[:, :HALF]
        o_all[2 * tile + 1] = o[:, HALF:]

    def give_back(kind, start):
        def step(j, carry):
            if kind == "corner":
                at, to_r, to_c, half = j, side * 24 + j, c, c
            elif kind == "edge":
                level = side == c
                at = CORNER + j
                to_r = jnp.where(level, side * 24 + lax.rem(j, 8), 8 + j)
                to_c = jnp.where(level, j // 8, c)
                half = jnp.where(level, 1 - to_c, to_c)
            else:
                at, to_r, to_c, half = CORNER + EDGE + j, 8 + 8 * side + j, c, 1 - c
            transfer(o_all.at[at], attended.at[frame, half, head], to_r, to_c, back_send_sem, back_sem, start)
            return carry

        lax.fori_loop(0, EDGE if kind == "edge" else 8, step, 0)

    score_pass(0, scores_a, max_a)

    def two_units(i, carry):
        @pl.when(i == 4)
        def _():
            arrived(own, own_sem)
            for b in range(OWN):
                take_kv(own[b], 24 + b, 16)
                take_q(own[b], 24 + b)
            arrived(other, other_sem)
            for b in range(OTHER):
                take_kv(other[b], 32 + b, 0)

        @pl.when(i == 5)
        def _():
            for tile in range(4):
                finish(tile, tile, 1)
            give_back("corner", True)
            for tile in range(8):
                finish(4 + tile, 4 + 2 * tile, 2)
            give_back("edge", True)

        score_pass(2 * i + 1, scores_b, max_b)
        value_pass(2 * i, scores_a, max_a)
        score_pass(jnp.minimum(2 * i + 2, UNITS - 1), scores_a, max_a)
        value_pass(2 * i + 1, scores_b, max_b)
        return carry

    lax.fori_loop(0, UNITS // 2, two_units, 0)
    for tile in range(4):
        finish(12 + tile, 20 + 4 * tile, 4)
    give_back("centre", True)

    send_all(False)
    for kind in ("corner", "edge", "centre"):
        give_back(kind, False)
    arrived(attended, back_sem)

    def refine(f, source):
        cells = jnp.concatenate(
            [source[:, 32 * half : 32 * half + 32, :].reshape(HALF, CHAN) for half in range(2)], axis=0
        )
        heads = jnp.concatenate(
            [attended[f, half].reshape(CHAN, HALF).astype(F32).T.astype(BF16) for half in range(2)], axis=0
        )
        message = layer_norm(nn(heads, merge_w[...]), message_gain[...], message_bias[...]).astype(BF16)
        joined = jnp.concatenate([cells, message], axis=1)
        update = jnp.zeros((2 * HALF, CHAN), F32)
        for j in range(HIDDEN // 256):
            hidden = erf_gelu(nn(joined, expand_w[:, 256 * j : 256 * j + 256])).astype(BF16)
            update = update + nn(hidden, reduce_w[256 * j : 256 * j + 256, :])
        return cells.astype(F32) + layer_norm(update, update_gain[...], update_bias[...])

    column, line = lax.rem(r, 8), r // 8

    def spread(kind, start):
        def step(i, carry):
            if kind == "k":
                to = lax.rem(line * 2 + c + i, GROUP)
                to_r, to_c, at, ref, sem = (to // 2) * 8 + column, lax.rem(to, 2), line * 2 + c, ref_k, k_sem
            else:
                to_r, to_c, at, ref, sem = line * 8 + lax.rem(column + i, GROUP), c, column, ref_q, q_sem
            copy = pltpu.make_async_remote_copy(
                ref.at[at], ref.at[at], ref_send_sem, sem, device_id=(pair, to_r, to_c), device_id_type=MESH
            )
            if start:
                copy.start()
            else:
                copy.wait_send()
            return carry

        lax.fori_loop(1, GROUP, step, 0)

    ref_k[line * 2 + c] = refine(1, second).astype(BF16)
    spread("k", True)
    ref_q[column] = (refine(0, first) * (LOG2E / math.sqrt(CHAN))).astype(BF16)
    spread("q", True)

    at = lax.broadcasted_iota(jnp.int32, (16, TILE), 1)
    what = lax.broadcasted_iota(jnp.int32, (16, TILE), 0)
    for k in range(GROUP):
        key_column = 64 * (k % 2) + 32 * (at // HALF) + at % 32
        key_row = 4 * (8 * (k // 2) + column) + (at // 32) % 4
        weigh = jnp.where(what == 0, 1, jnp.where(what == 1, key_column, key_row))
        where_v[:, TILE * k : TILE * (k + 1)] = weigh.astype(F32).astype(BF16)

    pltpu.make_async_copy(ref_k.at[0:7], ref_k.at[0:7], k_sem).wait()
    pltpu.make_async_copy(ref_q.at[0:7], ref_q.at[0:7], q_sem).wait()

    def corr_scores(t, scores, top):
        x = nt(ref_k[...].reshape(GROUP * TILE, CHAN), ref_q[t])
        scores[...] = x
        top[0] = jnp.max(x.reshape(GROUP * TILE // 8, 8, TILE), axis=0)

    def corr_sums(t, scores, top):
        m = jnp.max(top[0], axis=0, keepdims=True)
        p = jnp.exp2(scores[...] - m).astype(BF16)
        sums = nn(where_v[...], p)
        partial[t] = jnp.concatenate([sums[0:7], m], axis=0)

    corr_scores(0, scores_a, max_a)

    def two_tiles(i, carry):
        corr_scores(2 * i + 1, scores_b, max_b)
        corr_sums(2 * i, scores_a, max_a)
        corr_scores(jnp.minimum(2 * i + 2, GROUP - 1), scores_a, max_a)
        corr_sums(2 * i + 1, scores_b, max_b)
        return carry

    lax.fori_loop(0, GROUP // 2, two_tiles, 0)

    def hand_in(start):
        def step(i, carry):
            to = lax.rem(column + i, GROUP)
            copy = pltpu.make_async_remote_copy(
                partial.at[to], parts.at[column], part_send_sem, part_sem,
                device_id=(pair, line * 8 + to, c), device_id_type=MESH,
            )
            if start:
                copy.start()
            else:
                copy.wait_send()
            return carry

        lax.fori_loop(1, GROUP, step, 0)

    hand_in(True)
    parts[column] = partial[column]
    spread("k", False)
    spread("q", False)
    hand_in(False)
    pltpu.make_async_copy(parts.at[0:7], parts.at[0:7], part_sem).wait()

    m = jnp.max(parts[:, 7:8, :], axis=0)
    total = jnp.zeros((8, TILE), F32)
    for j in range(GROUP):
        total = total + parts[j] * jnp.exp2(parts[j, 7:8, :] - m)
    lane = lax.broadcasted_iota(jnp.int32, (1, TILE), 1)
    own_column = (64 * c + 32 * (lane // HALF) + lane % 32).astype(F32)
    own_row = (4 * r + (lane // 32) % 4).astype(F32)
    flows = (
        (total[1:2] / total[0:1] - own_column) * (2.0 / 128),
        (total[2:3] / total[0:1] - own_row) * (2.0 / 128),
    )
    for which in range(2):
        for i in range(4):
            for half in range(2):
                start = half * HALF + 32 * i
                out[which, i : i + 1, 32 * half : 32 * half + 32] = flows[which][:, start : start + 32]


def shards(first, second, attend_w, merge_w, message_gain, message_bias, expand_w, reduce_w, update_gain, update_bias):
    rows = [v.reshape(1, CHAN) for v in (message_gain, message_bias, update_gain, update_bias)]
    vmem = pl.BlockSpec(memory_space=pltpu.VMEM)
    dma = pltpu.SemaphoreType.DMA
    return pl.pallas_call(
        kernel,
        out_shape=jax.ShapeDtypeStruct((2, 4, 64), F32),
        in_specs=[vmem] * 10,
        out_specs=vmem,
        scratch_shapes=[
            pltpu.VMEM((2, 2, HEADS, 48, HALF), BF16),
            pltpu.VMEM((CORNER, 48, HALF), BF16),
            pltpu.VMEM((EDGE, 48, HALF), BF16),
            pltpu.VMEM((OWN, 48, HALF), BF16),
            pltpu.VMEM((OTHER, 32, HALF), BF16),
            pltpu.VMEM((16, 16, TILE), BF16),
            pltpu.VMEM((7 * CHUNK, 16), BF16),
            pltpu.VMEM((32, 7 * CHUNK), BF16),
            pltpu.VMEM((2 * CHUNK, TILE), F32),
            pltpu.VMEM((2 * CHUNK, TILE), F32),
            pltpu.VMEM((2, 8, TILE), F32),
            pltpu.VMEM((2, 8, TILE), F32),
            pltpu.VMEM((2 * UNITS, 32, TILE), F32),
            pltpu.VMEM((2 * UNITS, 8, TILE), F32),
            pltpu.VMEM((32, 16, HALF), BF16),
            pltpu.VMEM((2, 2, HEADS, 16, HALF), BF16),
            pltpu.VMEM((GROUP, TILE, CHAN), BF16),
            pltpu.VMEM((GROUP, TILE, CHAN), BF16),
            pltpu.VMEM((16, GROUP * TILE), BF16),
            pltpu.VMEM((GROUP, 8, TILE), F32),
            pltpu.VMEM((GROUP, 8, TILE), F32),
        ]
        + [dma] * 12,
        compiler_params=pltpu.CompilerParams(
            collective_id=0, has_side_effects=True, vmem_limit_bytes=40 * 1024 * 1024
        ),
    )(first, second, attend_w, merge_w, rows[0], rows[1], expand_w, reduce_w, rows[2], rows[3])


def solution(mesh):
    split = P(("pair", "row"), "col", None)
    return jax.shard_map(
        shards,
        mesh=mesh,
        in_specs=(split, split) + (P(),) * 8,
        out_specs=P(None, ("pair", "row"), "col"),
        check_vma=False,
    )
```

```python
import functools
import math

import jax
import jax.numpy as jnp
from jax import lax
from jax.experimental import pallas as pl
from jax.experimental.pallas import tpu as pltpu
from jax.sharding import PartitionSpec as P

HEADS = 8
HEAD_DIM = 16
CHAN = 128
HIDDEN = 1024
NORM_EPSILON = 1e-05
LOG2E = math.log2(math.e)
MESH = pl.DeviceIdType.MESH
F32 = jnp.float32
BF16 = jnp.bfloat16

HALF = 128
TILE = 512
CHUNK = 1024
PIECE = 256
CELLS = 256
CORNER, EDGE, OWN, OTHER = 8, 16, 8, 24
UNITS = 9
GROUP = 8


def nn(a, b):
    return jnp.dot(a, b, preferred_element_type=F32)


def nt(a, b):
    return lax.dot_general(a, b, (((1,), (1,)), ((), ())), preferred_element_type=F32)


def layer_norm(values, gain, bias):
    centre = values - jnp.mean(values, axis=-1, keepdims=True)
    spread = jnp.mean(centre * centre, axis=-1, keepdims=True)
    return centre * lax.rsqrt(spread + NORM_EPSILON) * gain + bias


def erf_gelu(x):
    return 0.5 * x * (1.0 + lax.erf(x * (1.0 / math.sqrt(2.0))))


def unit_tile(n):
    tile = jnp.where(n < 2, n, jnp.where(n < 10, 2 + (n - 2) // 2, 6 + (n - 10) // 4))
    chunk = jnp.where(n < 2, 0, jnp.where(n < 10, 1 + lax.rem(n, 2), 3 + lax.rem(n - 10, 4)))
    return tile, chunk


def kernel(*refs):
    inputs, out, held, refs = refs[:10], refs[10], refs[11:21], refs[21:]
    (first, second, attend_w, merge_w, message_gain, message_bias, expand_w, reduce_w, update_gain, update_bias) = held
    (
    sent, corner, edge, own, other,
    q_all, k_all, v_all, scores_a, scores_b, max_a, max_b, accs, maxes,
    o_all, attended, ref_q, ref_k, where_v, partial, parts,
    send_sem, corner_sem, edge_sem, own_sem, other_sem,
    back_send_sem, back_sem, ref_send_sem, q_sem, k_sem, part_send_sem, part_sem, k_far_sem, load_sem,
    ) = refs
    loads = [pltpu.make_async_copy(inputs[j], held[j], load_sem.at[j]) for j in range(10)]
    for j in (0, 1, 2, 3, 4, 5, 6, 7, 8, 9):
        loads[j].start()
    pair, r, c = lax.axis_index("pair"), lax.axis_index("row"), lax.axis_index("col")
    me = r * 2 + c
    side = r // 16
    place = lax.rem(r, 16)
    head, frame = place // 2, lax.rem(place, 2)
    middle = (r >= 8) & (r < 24)

    barrier = pltpu.get_barrier_semaphore()

    def greet(i, carry):
        peer = lax.rem(me + 1 + i, 64)
        pl.semaphore_signal(barrier, inc=1, device_id=(pair, peer // 2, lax.rem(peer, 2)), device_id_type=MESH)
        return carry

    lax.fori_loop(0, 63, greet, 0)

    for j in (0, 1, 2):
        loads[j].wait()

    weight_t = attend_w[...].T
    for f, source in enumerate((first, second)):
        for half in range(2):
            cells = source[:, 32 * half : 32 * half + 32, :].reshape(HALF, CHAN)
            projected = nt(weight_t, cells)
            queries = projected[:CHAN] * (LOG2E / math.sqrt(HEAD_DIM))
            sent[f, half, :, 0:16, :] = queries.astype(BF16).reshape(HEADS, 16, HALF)
            sent[f, half, :, 16:32, :] = projected[CHAN : 2 * CHAN].astype(BF16).reshape(HEADS, 16, HALF)
            sent[f, half, :, 32:48, :] = projected[2 * CHAN :].astype(BF16).reshape(HEADS, 16, HALF)

    pl.semaphore_wait(barrier, 63)

    def transfer(source, target, dest_r, dest_c, s_sem, r_sem, start):
        here = (dest_r == r) & (dest_c == c)

        @pl.when(jnp.logical_not(here))
        def _():
            copy = pltpu.make_async_remote_copy(
                source, target, s_sem, r_sem, device_id=(pair, dest_r, dest_c), device_id_type=MESH
            )
            if start:
                copy.start()
            else:
                copy.wait_send()

        if start:

            @pl.when(here)
            def _():
                pltpu.make_async_copy(source, target, r_sem).start()

    def send_all(start):
        def each(body):
            def step(i, carry):
                d = lax.rem(place + i, 16)
                body(d // 2, lax.rem(d, 2), d)
                return carry

            lax.fori_loop(0, 16, step, 0)

        inner = 1 - c

        @pl.when(middle)
        def _():
            def outer_half(h, f, d):
                transfer(sent.at[f, c, h], edge.at[r - 8], (1 - c) * 16 + d, c, send_sem, edge_sem, start)

            def own_half(h, f, d):
                transfer(sent.at[f, inner, h], own.at[lax.rem(r, 8)], side * 16 + d, c, send_sem, own_sem, start)

            def other_halves(h, f, d):
                for turn in range(1, 4):
                    to_side, to_c = side ^ (turn // 2), c ^ (turn % 2)
                    transfer(
                        sent.at[f, inner, h, 16:48],
                        other.at[(turn - 1) * 8 + lax.rem(r, 8)],
                        to_side * 16 + d, to_c, send_sem, other_sem, start,
                    )

            each(outer_half)
            each(own_half)
            each(other_halves)

        @pl.when(jnp.logical_not(middle))
        def _():
            def corner_half(h, f, d):
                transfer(sent.at[f, c, h], corner.at[lax.rem(r, 8)], side * 16 + d, c, send_sem, corner_sem, start)

            def edge_half(h, f, d):
                slot = c * 8 + lax.rem(r, 8)
                transfer(sent.at[f, inner, h], edge.at[slot], side * 16 + d, side, send_sem, edge_sem, start)

            each(corner_half)
            each(edge_half)

    send_all(True)

    def arrived(ref, sem):
        pltpu.make_async_copy(ref, ref, sem).wait()

    def take_kv(block, at, first_row):
        k_all[at * HALF : (at + 1) * HALF, :] = block[first_row : first_row + 16, :].astype(F32).T.astype(BF16)
        v_all[0:16, at * HALF : (at + 1) * HALF] = block[first_row + 16 : first_row + 32, :]

    def take_q(block, at):
        q_all[at // 4, :, (at % 4) * HALF : (at % 4 + 1) * HALF] = block[0:16, :]

    def together(score, value):
        for sub in range(2):
            if score:
                scores, top, get_queries, get_keys = score
                queries = get_queries(sub)
                largest = jnp.full((8, TILE), -jnp.inf, F32)
            if value:
                lifted, tops, get_values, put = value
                m = jnp.max(tops[sub], axis=0, keepdims=True)
                acc = None
            for j in range(CHUNK // PIECE):
                at = slice(sub * CHUNK + j * PIECE, sub * CHUNK + (j + 1) * PIECE)
                if score:
                    x = get_keys(sub, j, queries)
                    scores[at, :] = x
                    largest = jnp.maximum(largest, jnp.max(x.reshape(PIECE // 8, 8, TILE), axis=0))
                if value:
                    p = jnp.exp2(lifted[at, :] - m).astype(BF16)
                    product = nn(get_values(sub, j), p)
                    acc = product if acc is None else acc + product
            if score:
                top[sub] = largest
            if value:
                put(sub, m, acc)

    held_scores = ((scores_a, max_a), (scores_b, max_b))

    def attend_score(u, slot):
        def get_queries(sub):
            return q_all[unit_tile(2 * u + sub)[0]]

        def get_scores(sub, j, queries):
            first_key = unit_tile(2 * u + sub)[1] * CHUNK + j * PIECE
            return nn(k_all[pl.ds(pl.multiple_of(first_key, PIECE), PIECE), :], queries)

        return (*held_scores[slot], get_queries, get_scores)

    def attend_value(u, slot):
        def get_values(sub, j):
            first_key = unit_tile(2 * u + sub)[1] * CHUNK + j * PIECE
            return v_all[:, pl.ds(pl.multiple_of(first_key, PIECE), PIECE)]

        def put(sub, m, acc):
            accs[2 * u + sub] = acc
            maxes[2 * u + sub] = jnp.broadcast_to(m, (8, TILE))

        return (*held_scores[slot], get_values, put)

    v_all[16:32, :] = jnp.ones_like(v_all[16:32, :])
    arrived(corner, corner_sem)
    for b in range(CORNER):
        take_kv(corner[b], b, 16)
        take_q(corner[b], b)
    together(attend_score(0, 0), None)
    arrived(edge, edge_sem)
    for b in range(EDGE):
        take_kv(edge[b], 8 + b, 16)
        take_q(edge[b], 8 + b)

    def finish(tile, n, count):
        m = maxes[n, 0:1]
        for j in range(1, count):
            m = jnp.maximum(m, maxes[n + j, 0:1])
        acc = accs[n] * jnp.exp2(maxes[n, 0:1] - m)
        for j in range(1, count):
            acc = acc + accs[n + j] * jnp.exp2(maxes[n + j, 0:1] - m)
        o = (acc[0:16] / acc[16:17]).astype(BF16)
        for b in range(4):
            o_all[4 * tile + b] = o[:, b * HALF : (b + 1) * HALF]

    def give_back(kind, start):
        def step(j, carry):
            if kind == "corner":
                at, to_r, to_c, half = j, side * 24 + j, c, c
            elif kind == "edge":
                level = side == c
                at = CORNER + j
                to_r = jnp.where(level, side * 24 + lax.rem(j, 8), 8 + j)
                to_c = jnp.where(level, j // 8, c)
                half = jnp.where(level, 1 - to_c, to_c)
            else:
                at, to_r, to_c, half = CORNER + EDGE + j, 8 + 8 * side + j, c, 1 - c
            transfer(o_all.at[at], attended.at[frame, half, head], to_r, to_c, back_send_sem, back_sem, start)
            return carry

        lax.fori_loop(0, EDGE if kind == "edge" else 8, step, 0)

    def two_units(i, carry):
        @pl.when(i == 2)
        def _():
            arrived(own, own_sem)
            for b in range(OWN):
                take_kv(own[b], 24 + b, 16)
                take_q(own[b], 24 + b)
            arrived(other, other_sem)
            for b in range(OTHER):
                take_kv(other[b], 32 + b, 0)

        together(attend_score(2 * i + 1, 1), attend_value(2 * i, 0))

        @pl.when(i == 2)
        def _():
            for tile in range(2):
                finish(tile, tile, 1)
            give_back("corner", True)
            for tile in range(4):
                finish(2 + tile, 2 + 2 * tile, 2)
            give_back("edge", True)

        together(attend_score(2 * i + 2, 0), attend_value(2 * i + 1, 1))
        return carry

    lax.fori_loop(0, UNITS // 2, two_units, 0)
    together(None, attend_value(UNITS - 1, 0))
    for tile in range(2):
        finish(6 + tile, 10 + 4 * tile, 4)
    give_back("centre", True)

    send_all(False)
    for kind in ("corner", "edge", "centre"):
        give_back(kind, False)
    arrived(attended, back_sem)
    for j in range(3, 10):
        loads[j].wait()

    def refine(f, source):
        cells = jnp.concatenate(
            [source[:, 32 * half : 32 * half + 32, :].reshape(HALF, CHAN) for half in range(2)], axis=0
        )
        heads = jnp.concatenate(
            [attended[f, half].reshape(CHAN, HALF).astype(F32).T.astype(BF16) for half in range(2)], axis=0
        )
        message = layer_norm(nn(heads, merge_w[...]), message_gain[...], message_bias[...]).astype(BF16)
        joined = jnp.concatenate([cells, message], axis=1)
        update = jnp.zeros((2 * HALF, CHAN), F32)
        for j in range(HIDDEN // 256):
            hidden = erf_gelu(nn(joined, expand_w[:, 256 * j : 256 * j + 256])).astype(BF16)
            update = update + nn(hidden, reduce_w[256 * j : 256 * j + 256, :])
        return cells.astype(F32) + layer_norm(update, update_gain[...], update_bias[...])

    column, line = lax.rem(r, 8), r // 8

    def spread(kind, start):
        def step(i, carry):
            if kind == "k":
                to_line, to_c = lax.rem(line + i // 2, 4), c ^ lax.rem(i, 2)
                at = lax.rem(4 - i // 2, 4) * 2 + lax.rem(i, 2)
                for near in (True, False):

                    @pl.when((at < 4) == near)
                    def _():
                        copy = pltpu.make_async_remote_copy(
                            ref_k.at[0], ref_k.at[at], ref_send_sem, k_sem if near else k_far_sem,
                            device_id=(pair, to_line * 8 + column, to_c), device_id_type=MESH,
                        )
                        if start:
                            copy.start()
                        else:
                            copy.wait_send()
            else:
                copy = pltpu.make_async_remote_copy(
                    ref_q.at[column], ref_q.at[column], ref_send_sem, q_sem,
                    device_id=(pair, line * 8 + lax.rem(column + i, GROUP), c), device_id_type=MESH,
                )
                if start:
                    copy.start()
                else:
                    copy.wait_send()
            return carry

        lax.fori_loop(1, GROUP, step, 0)

    ref_k[0] = refine(1, second).astype(BF16)
    spread("k", True)
    ref_q[column] = (refine(0, first) * (LOG2E / math.sqrt(CHAN))).astype(BF16)
    spread("q", True)

    at = lax.broadcasted_iota(jnp.int32, (16, CELLS), 1)
    what = lax.broadcasted_iota(jnp.int32, (16, CELLS), 0)
    for k in range(GROUP):
        key_column = 64 * (c ^ (k % 2)) + 32 * (at // HALF) + at % 32
        key_row = 4 * (8 * lax.rem(line + k // 2, 4) + column) + (at // 32) % 4
        weigh = jnp.where(what == 0, 1, jnp.where(what == 1, key_column, key_row))
        where_v[:, CELLS * k : CELLS * (k + 1)] = weigh.astype(F32).astype(BF16)

    def corr_score(u, slot):
        def get_queries(sub):
            t = (2 * u + sub) % 4
            return ref_q[2 * t : 2 * t + 2].reshape(TILE, CHAN)

        def get_scores(sub, j, queries):
            return nt(ref_k[(2 * u + sub) // 4 * 4 + j], queries)

        return (*held_scores[slot], get_queries, get_scores)

    def corr_value(u, slot):
        def get_values(sub, j):
            k = (2 * u + sub) // 4 * 4 + j
            return where_v[:, CELLS * k : CELLS * (k + 1)]

        def put(sub, m, acc):
            chunk, t = (2 * u + sub) // 4, (2 * u + sub) % 4
            sums = jnp.concatenate([acc[0:7], m], axis=0)
            partial[chunk, 2 * t] = sums[:, :CELLS]
            partial[chunk, 2 * t + 1] = sums[:, CELLS:]

        return (*held_scores[slot], get_values, put)

    def hand_in(u, start):
        chunk = u // 2

        def step(i, carry):
            to = 4 * (u % 2) + i
            copy = pltpu.make_async_remote_copy(
                partial.at[chunk, to], parts.at[chunk * GROUP + column], part_send_sem, part_sem,
                device_id=(pair, line * 8 + to, c), device_id_type=MESH,
            )

            @pl.when(to != column)
            def _():
                if start:
                    copy.start()
                else:
                    copy.wait_send()

            if start:

                @pl.when(to == column)
                def _():
                    pltpu.make_async_copy(partial.at[chunk, to], parts.at[chunk * GROUP + column], part_sem).start()

            return carry

        lax.fori_loop(0, 4, step, 0)

    pltpu.make_async_copy(ref_q.at[0:7], ref_q.at[0:7], q_sem).wait()
    pltpu.make_async_copy(ref_k.at[1:4], ref_k.at[1:4], k_sem).wait()
    together(corr_score(0, 0), None)
    together(corr_score(1, 1), corr_value(0, 0))
    hand_in(0, True)
    pltpu.make_async_copy(ref_k.at[4:8], ref_k.at[4:8], k_far_sem).wait()
    together(corr_score(2, 0), corr_value(1, 1))
    hand_in(1, True)
    together(corr_score(3, 1), corr_value(2, 0))
    hand_in(2, True)
    together(None, corr_value(3, 1))
    hand_in(3, True)
    spread("k", False)
    spread("q", False)
    for u in range(4):
        hand_in(u, False)
    arrived(parts, part_sem)

    m = jnp.max(parts[:, 7:8, :], axis=0)
    total = jnp.zeros((8, CELLS), F32)
    for j in range(2 * GROUP):
        total = total + parts[j] * jnp.exp2(parts[j, 7:8, :] - m)
    lane = lax.broadcasted_iota(jnp.int32, (1, CELLS), 1)
    own_column = (64 * c + 32 * (lane // HALF) + lane % 32).astype(F32)
    own_row = (4 * r + (lane // 32) % 4).astype(F32)
    flows = (
        (total[1:2] / total[0:1] - own_column) * (2.0 / 128),
        (total[2:3] / total[0:1] - own_row) * (2.0 / 128),
    )
    for which in range(2):
        for i in range(4):
            for half in range(2):
                start = half * HALF + 32 * i
                out[which, i : i + 1, 32 * half : 32 * half + 32] = flows[which][:, start : start + 32]


def shards(first, second, attend_w, merge_w, message_gain, message_bias, expand_w, reduce_w, update_gain, update_bias):
    rows = [v.reshape(1, CHAN) for v in (message_gain, message_bias, update_gain, update_bias)]
    operands = (first, second, attend_w, merge_w, rows[0], rows[1], expand_w, reduce_w, rows[2], rows[3])
    vmem = pl.BlockSpec(memory_space=pltpu.VMEM)
    dma = pltpu.SemaphoreType.DMA
    return pl.pallas_call(
        kernel,
        out_shape=jax.ShapeDtypeStruct((2, 4, 64), F32),
        in_specs=[pl.BlockSpec(memory_space=pl.ANY)] * 10,
        out_specs=vmem,
        scratch_shapes=[pltpu.VMEM(v.shape, v.dtype) for v in operands]
        + [
            pltpu.VMEM((2, 2, HEADS, 48, HALF), BF16),
            pltpu.VMEM((CORNER, 48, HALF), BF16),
            pltpu.VMEM((EDGE, 48, HALF), BF16),
            pltpu.VMEM((OWN, 48, HALF), BF16),
            pltpu.VMEM((OTHER, 32, HALF), BF16),
            pltpu.VMEM((8, 16, TILE), BF16),
            pltpu.VMEM((7 * CHUNK, 16), BF16),
            pltpu.VMEM((32, 7 * CHUNK), BF16),
            pltpu.VMEM((2 * CHUNK, TILE), F32),
            pltpu.VMEM((2 * CHUNK, TILE), F32),
            pltpu.VMEM((2, 8, TILE), F32),
            pltpu.VMEM((2, 8, TILE), F32),
            pltpu.VMEM((2 * UNITS, 32, TILE), F32),
            pltpu.VMEM((2 * UNITS, 8, TILE), F32),
            pltpu.VMEM((32, 16, HALF), BF16),
            pltpu.VMEM((2, 2, HEADS, 16, HALF), BF16),
            pltpu.VMEM((GROUP, CELLS, CHAN), BF16),
            pltpu.VMEM((GROUP, CELLS, CHAN), BF16),
            pltpu.VMEM((16, GROUP * CELLS), BF16),
            pltpu.VMEM((2, GROUP, 8, CELLS), F32),
            pltpu.VMEM((2 * GROUP, 8, CELLS), F32),
        ]
        + [dma] * 13
        + [dma((10,))],
        compiler_params=pltpu.CompilerParams(
            collective_id=0, has_side_effects=True, vmem_limit_bytes=67000000
        ),
    )(*operands)


def solution(mesh):
    split = P(("pair", "row"), "col", None)
    return jax.shard_map(
        shards,
        mesh=mesh,
        in_specs=(split, split) + (P(),) * 8,
        out_specs=P(None, ("pair", "row"), "col"),
        check_vma=False,
    )
```

```python
import functools
import math

import jax
import jax.numpy as jnp
from jax import lax
from jax.experimental import pallas as pl
from jax.experimental.pallas import tpu as pltpu
from jax.sharding import PartitionSpec as P

HEADS = 8
HEAD_DIM = 16
CHAN = 128
HIDDEN = 1024
NORM_EPSILON = 1e-05
LOG2E = math.log2(math.e)
MESH = pl.DeviceIdType.MESH
F32 = jnp.float32
BF16 = jnp.bfloat16

HALF = 128
TILE = 512
CHUNK = 1024
PIECE = 256
CELLS = 256
CORNER, EDGE, OWN, OTHER = 8, 16, 8, 24
UNITS = 9
ORDER = (0, 1, 3, 2)
GROUP = 8


def nn(a, b):
    return jnp.dot(a, b, preferred_element_type=F32)


def nt(a, b):
    return lax.dot_general(a, b, (((1,), (1,)), ((), ())), preferred_element_type=F32)


def layer_norm(values, gain, bias):
    centre = values - jnp.mean(values, axis=-1, keepdims=True)
    spread = jnp.mean(centre * centre, axis=-1, keepdims=True)
    return centre * lax.rsqrt(spread + NORM_EPSILON) * gain + bias


def erf_gelu(x):
    return 0.5 * x * (1.0 + lax.erf(x * (1.0 / math.sqrt(2.0))))


def unit_tile(n):
    tile = jnp.where(n < 2, n, jnp.where(n < 10, 2 + (n - 2) // 2, 6 + (n - 10) // 4))
    chunk = jnp.where(n < 2, 0, jnp.where(n < 10, 1 + lax.rem(n, 2), 3 + lax.rem(n - 10, 4)))
    return tile, chunk


def kernel(*refs):
    inputs, out, held, refs = refs[:10], refs[10], refs[11:21], refs[21:]
    (first, second, attend_w, merge_w, message_gain, message_bias, expand_w, reduce_w, update_gain, update_bias) = held
    (
    sent, corner, edge, own, other,
    q_all, k_all, v_all, scores_a, scores_b, max_a, max_b, accs, maxes,
    o_all, attended, ref_q, ref_k, where_v, running, partial, parts,
    send_sem, corner_sem, edge_sem, own_sem, other_sem,
    back_send_sem, back_sem, ref_send_sem, q_sem, k_sem, part_send_sem, part_sem, load_sem, core_sem,
    relay_send_sem, relay_sem, q_pass_send_sem, q_pass_sem,
    ) = refs
    loads = [pltpu.make_async_copy(inputs[j], held[j], load_sem.at[j]) for j in range(10)]
    for j in (0, 1, 2, 3, 4, 5, 6, 7, 8, 9):
        loads[j].start()
    pair, r, c = lax.axis_index("pair"), lax.axis_index("row"), lax.axis_index("col")
    place, side = r >> 1, r & 1
    head, frame = place >> 1, place & 1
    own_side = r >> 4
    middle = (r >= 8) & (r < 24)

    barrier = pltpu.get_barrier_semaphore()

    def greet(i, carry):
        to = (r >> 1) * 2 + c + 1 + i & 31
        pl.semaphore_signal(barrier, inc=1, device_id=(pair, (to >> 1) * 2 + (r & 1), to & 1), device_id_type=MESH)
        return carry

    pl.semaphore_signal(barrier, inc=1, device_id=(pair, r ^ 1, c), device_id_type=MESH)
    lax.fori_loop(0, 31, greet, 0, unroll=True)

    for j in (0, 1, 2):
        loads[j].wait()

    weight_t = attend_w[...].T
    for f, source in enumerate((first, second)):
        for half in range(2):
            cells = source[:, 32 * half : 32 * half + 32, :].reshape(HALF, CHAN)
            projected = nt(weight_t, cells)
            queries = projected[:CHAN] * (LOG2E / math.sqrt(HEAD_DIM))
            sent[f, half, :, 0:16, :] = queries.astype(BF16).reshape(HEADS, 16, HALF)
            sent[f, half, :, 16:32, :] = projected[CHAN : 2 * CHAN].astype(BF16).reshape(HEADS, 16, HALF)
            sent[f, half, :, 32:48, :] = projected[2 * CHAN :].astype(BF16).reshape(HEADS, 16, HALF)

    pl.semaphore_wait(barrier, 32)
    pl.semaphore_signal(core_sem, inc=1, device_id=(pair, r ^ 1, c), device_id_type=MESH)
    pl.semaphore_wait(core_sem, 1)

    def transfer(source, target, dest_r, dest_c, s_sem, r_sem, start):
        here = (dest_r == r) & (dest_c == c)

        @pl.when(jnp.logical_not(here))
        def _():
            copy = pltpu.make_async_remote_copy(
                source, target, s_sem, r_sem, device_id=(pair, dest_r, dest_c), device_id_type=MESH
            )
            if start:
                copy.start()
            else:
                copy.wait_send()

        if start:

            @pl.when(here)
            def _():
                pltpu.make_async_copy(source, target, r_sem).start()

    def send_all(start):
        def each(body):
            def step(i, carry):
                d = place + i & 15
                body(d >> 1, d & 1, d)
                return carry

            lax.fori_loop(0, 16, step, 0, unroll=4 if start else 1)

        inner = 1 - c

        @pl.when(middle)
        def _():
            def outer_half(h, f, d):
                transfer(sent.at[f, c, h], edge.at[r - 8], d * 2 + 1 - c, c, send_sem, edge_sem, start)

            def own_half(h, f, d):
                transfer(sent.at[f, inner, h], own.at[r & 7], d * 2 + own_side, c, send_sem, own_sem, start)

            def other_half(h, f, d):
                transfer(
                    sent.at[f, inner, h, 16:48], other.at[r & 7], d * 2 + own_side, 1 - c, send_sem, other_sem, start
                )

            each(outer_half)
            each(own_half)
            each(other_half)

        @pl.when(jnp.logical_not(middle))
        def _():
            def corner_half(h, f, d):
                transfer(sent.at[f, c, h], corner.at[r & 7], d * 2 + own_side, c, send_sem, corner_sem, start)

            def edge_half(h, f, d):
                slot = c * 8 + (r & 7)
                transfer(sent.at[f, inner, h], edge.at[slot], d * 2 + own_side, own_side, send_sem, edge_sem, start)

            each(corner_half)
            each(edge_half)

    send_all(True)

    relays = [
        pltpu.make_async_remote_copy(
            source, target, relay_send_sem, relay_sem, device_id=(pair, r ^ 1, c), device_id_type=MESH
        )
        for source, target in ((own.at[:, 16:48], other.at[8:16]), (other.at[0:8], other.at[16:24]))
    ]

    def arrived(ref, sem):
        pltpu.make_async_copy(ref, ref, sem).wait()

    def take_kv(block, at, first_row):
        k_all[at * HALF : (at + 1) * HALF, :] = block[first_row : first_row + 16, :].astype(F32).T.astype(BF16)
        v_all[0:16, at * HALF : (at + 1) * HALF] = block[first_row + 16 : first_row + 32, :]

    def take_q(block, at):
        q_all[at // 4, :, (at % 4) * HALF : (at % 4 + 1) * HALF] = block[0:16, :]

    def together(score, value, tiles=2, chunk=CHUNK):
        for sub in range(tiles):
            if score:
                scores, top, get_queries, get_keys = score
                queries = get_queries(sub)
                largest = jnp.full((8, TILE), -jnp.inf, F32)
            if value:
                lifted, tops, get_values, put = value
                m = jnp.max(tops[sub], axis=0, keepdims=True)
                acc = None
            for j in range(chunk // PIECE):
                at = slice(sub * chunk + j * PIECE, sub * chunk + (j + 1) * PIECE)
                if score:
                    x = get_keys(sub, j, queries)
                    scores[at, :] = x
                    largest = jnp.maximum(largest, jnp.max(x.reshape(PIECE // 8, 8, TILE), axis=0))
                if value:
                    p = jnp.exp2(lifted[at, :] - m).astype(BF16)
                    product = nn(get_values(sub, j), p)
                    acc = product if acc is None else acc + product
            if score:
                top[sub] = largest
            if value:
                put(sub, m, acc)

    held_scores = ((scores_a, max_a), (scores_b, max_b))

    def attend_score(u, slot):
        def get_queries(sub):
            return q_all[unit_tile(2 * u + sub)[0]]

        def get_scores(sub, j, queries):
            first_key = unit_tile(2 * u + sub)[1] * CHUNK + j * PIECE
            return nn(k_all[pl.ds(pl.multiple_of(first_key, PIECE), PIECE), :], queries)

        return (*held_scores[slot], get_queries, get_scores)

    def attend_value(u, slot):
        def get_values(sub, j):
            first_key = unit_tile(2 * u + sub)[1] * CHUNK + j * PIECE
            return v_all[:, pl.ds(pl.multiple_of(first_key, PIECE), PIECE)]

        def put(sub, m, acc):
            accs[2 * u + sub] = acc
            maxes[2 * u + sub] = jnp.broadcast_to(m, (8, TILE))

        return (*held_scores[slot], get_values, put)

    v_all[16:32, :] = jnp.ones_like(v_all[16:32, :])
    arrived(corner, corner_sem)
    for b in range(CORNER):
        take_kv(corner[b], b, 16)
        take_q(corner[b], b)
    together(attend_score(0, 0), None)
    arrived(edge, edge_sem)
    for b in range(EDGE):
        take_kv(edge[b], 8 + b, 16)
        take_q(edge[b], 8 + b)

    def finish(tile, n, count):
        m = maxes[n, 0:1]
        for j in range(1, count):
            m = jnp.maximum(m, maxes[n + j, 0:1])
        acc = accs[n] * jnp.exp2(maxes[n, 0:1] - m)
        for j in range(1, count):
            acc = acc + accs[n + j] * jnp.exp2(maxes[n + j, 0:1] - m)
        o = (acc[0:16] / acc[16:17]).astype(BF16)
        for b in range(4):
            o_all[4 * tile + b] = o[:, b * HALF : (b + 1) * HALF]

    def give_back(kind, start, first=0, count=8):
        def step(j, carry):
            j = j + first
            if kind == "corner":
                at, to_r, to_c, half = j, side * 24 + j, c, c
            elif kind == "edge":
                level = side == c
                at = CORNER + j
                to_r = jnp.where(level, side * 24 + (j & 7), 8 + j)
                to_c = jnp.where(level, j >> 3, c)
                half = jnp.where(level, 1 - to_c, to_c)
            else:
                at, to_r, to_c, half = CORNER + EDGE + j, 8 + 8 * side + j, c, 1 - c
            transfer(o_all.at[at], attended.at[frame, half, head], to_r, to_c, back_send_sem, back_sem, start)
            return carry

        lax.fori_loop(0, count, step, 0, unroll=True if start else 1)

    def two_units(i, carry):
        @pl.when(i == 2)
        def _():
            for b in range(8):
                take_kv(other[b], 32 + b, 0)
            arrived(other.at[8:24], relay_sem)
            for b in range(8, OTHER):
                take_kv(other[b], 32 + b, 0)

        together(attend_score(2 * i + 1, 1), attend_value(2 * i, 0))

        @pl.when(i == 1)
        def _():
            arrived(own, own_sem)
            arrived(other.at[0:8], other_sem)
            for copy in relays:
                copy.start()
            for b in range(OWN):
                take_kv(own[b], 24 + b, 16)
                take_q(own[b], 24 + b)

        @pl.when(i == 2)
        def _():
            for tile in range(2):
                finish(tile, tile, 1)
            give_back("corner", True)
            for tile in range(4):
                finish(2 + tile, 2 + 2 * tile, 2)
            give_back("edge", True, 0, 16)

        together(attend_score(2 * i + 2, 0), attend_value(2 * i + 1, 1))
        return carry

    lax.fori_loop(0, UNITS // 2, two_units, 0)
    finish(6, 10, 4)
    give_back("centre", True, 0, 4)
    together(None, attend_value(UNITS - 1, 0))
    finish(7, 14, 4)
    give_back("centre", True, 4, 4)
    arrived(attended, back_sem)
    for j in range(3, 10):
        loads[j].wait()

    def refine(f, source):
        cells = jnp.concatenate(
            [source[:, 32 * half : 32 * half + 32, :].reshape(HALF, CHAN) for half in range(2)], axis=0
        )
        heads = jnp.concatenate(
            [attended[f, half].reshape(CHAN, HALF).astype(F32).T.astype(BF16) for half in range(2)], axis=0
        )
        message = layer_norm(nn(heads, merge_w[...]), message_gain[...], message_bias[...]).astype(BF16)
        joined = jnp.concatenate([cells, message], axis=1)
        update = jnp.zeros((2 * HALF, CHAN), F32)
        for j in range(HIDDEN // 256):
            hidden = erf_gelu(nn(joined, expand_w[:, 256 * j : 256 * j + 256])).astype(BF16)
            update = update + nn(hidden, reduce_w[256 * j : 256 * j + 256, :])
        return cells.astype(F32) + layer_norm(update, update_gain[...], update_bias[...])

    column, line = r & 7, r >> 3

    def spread(kind, start):
        def step(i, carry):
            if kind == "k":
                to_line, to_c = line + (i >> 1) & 3, c ^ (i & 1)
                at = (4 - (i >> 1) & 3) * 2 + (i & 1)
                ref, sem, to_r = ref_k, k_sem.at[at >> 1], to_line * 8 + column
            else:
                to_c, at = c, (4 - (i >> 1) & 3) * 2 + (i & 1)
                ref, sem, to_r = ref_q, q_pass_sem.at[0] if i == 1 else q_sem.at[at >> 1], line * 8 + ((column >> 1) + (i >> 1) & 3) * 2 + (column & 1 ^ i & 1)
            copy = pltpu.make_async_remote_copy(
                ref.at[0], ref.at[at], ref_send_sem, sem, device_id=(pair, to_r, to_c), device_id_type=MESH
            )
            if start:
                copy.start()
            else:
                copy.wait_send()
            return carry

        if start:
            for i in (1, 2, 3, 6, 7, 4, 5) if kind == "k" else (1, 2, 6, 4):
                step(i, 0)
        else:
            for i in range(1, GROUP) if kind == "k" else (1, 2, 6, 4):
                step(i, 0)

    ref_k[0] = refine(1, second).astype(BF16)
    spread("k", True)
    ref_q[0] = (refine(0, first) * (LOG2E / math.sqrt(CHAN))).astype(BF16)
    spread("q", True)

    at = lax.broadcasted_iota(jnp.int32, (16, CELLS), 1)
    what = lax.broadcasted_iota(jnp.int32, (16, CELLS), 0)
    for k in range(GROUP):
        key_column = 64 * (c ^ (k % 2)) + 32 * (at // HALF) + at % 32
        key_row = 4 * (8 * (line + k // 2 & 3) + column) + (at // 32) % 4
        weigh = jnp.where(what == 0, 1, jnp.where(what == 1, key_column, key_row))
        where_v[:, CELLS * k : CELLS * (k + 1)] = weigh.astype(F32).astype(BF16)

    def corr_score(u, slot):
        def get_queries(sub):
            t = ORDER[sub]
            if u == 0:
                arrived(ref_q.at[2 * t + 1], q_pass_sem.at[t])
            return ref_q[2 * t : 2 * t + 2].reshape(TILE, CHAN)

        def get_scores(sub, j, queries):
            return nt(ref_k[2 * ORDER[u] + j], queries)

        return (*held_scores[slot], get_queries, get_scores)

    def corr_value(u, slot):
        def get_values(sub, j):
            k = 2 * ORDER[u] + j
            return where_v[:, CELLS * k : CELLS * (k + 1)]

        def put(sub, m, acc):
            sums = acc[0:8]
            if u:
                before, m_before = running[sub, 0:8], running[sub, 8:9]
                m_now = jnp.maximum(m, m_before)
                sums = sums * jnp.exp2(m - m_now) + before * jnp.exp2(m_before - m_now)
                m = m_now
            if u < 3:
                running[sub, 0:8] = sums
                running[sub, 8:16] = jnp.broadcast_to(m, (8, TILE))
            else:
                sums = jnp.concatenate([sums[0:7], m], axis=0)
                partial[2 * sub] = sums[:, :CELLS]
                partial[2 * sub + 1] = sums[:, CELLS:]
                hand_in(sub, True)

        return (*held_scores[slot], get_values, put)

    def hand_in(sub, start):
        for i in range(2):
            at = 2 * ORDER[sub] + i
            if at == 0:
                if start:
                    parts[0] = partial[0]
                continue
            to = ((column >> 1) + ORDER[sub] & 3) * 2 + (column & 1 ^ i)
            copy = pltpu.make_async_remote_copy(
                partial.at[2 * sub + i], parts.at[(4 - ORDER[sub]) % 4 * 2 + i], part_send_sem, part_sem,
                device_id=(pair, line * 8 + to, c), device_id_type=MESH,
            )
            if start:
                copy.start()
            else:
                copy.wait_send()

    passes = []
    for t in ORDER[1:]:
        arrived(ref_q.at[2 * t], q_sem.at[t])
        copy = pltpu.make_async_remote_copy(
            ref_q.at[2 * t], ref_q.at[2 * t + 1], q_pass_send_sem, q_pass_sem.at[t],
            device_id=(pair, r ^ 1, c), device_id_type=MESH,
        )
        copy.start()
        passes.append(copy)

    def corr(score, value):
        together(score, value, tiles=4, chunk=2 * CELLS)

    arrived(ref_k.at[1:2], k_sem.at[0])
    corr(corr_score(0, 0), None)
    for u in range(1, 4):
        arrived(ref_k.at[2 * ORDER[u] : 2 * ORDER[u] + 2], k_sem.at[ORDER[u]])
        corr(corr_score(u, u % 2), corr_value(u - 1, (u - 1) % 2))
    corr(None, corr_value(3, 1))
    for copy in relays:
        copy.wait_send()
    send_all(False)
    give_back("corner", False)
    give_back("edge", False, 0, 16)
    give_back("centre", False)
    spread("k", False)
    spread("q", False)
    for copy in passes:
        copy.wait_send()
    for sub in range(4):
        hand_in(sub, False)
    arrived(parts.at[1:8], part_sem)

    m = jnp.max(parts[:, 7:8, :], axis=0)
    total = jnp.zeros((8, CELLS), F32)
    for j in range(GROUP):
        total = total + parts[j] * jnp.exp2(parts[j, 7:8, :] - m)
    lane = lax.broadcasted_iota(jnp.int32, (1, CELLS), 1)
    own_column = (64 * c + 32 * (lane // HALF) + lane % 32).astype(F32)
    own_row = (4 * r + (lane // 32) % 4).astype(F32)
    flows = (
        (total[1:2] / total[0:1] - own_column) * (2.0 / 128),
        (total[2:3] / total[0:1] - own_row) * (2.0 / 128),
    )
    for which in range(2):
        for i in range(4):
            for half in range(2):
                start = half * HALF + 32 * i
                out[which, i : i + 1, 32 * half : 32 * half + 32] = flows[which][:, start : start + 32]


def shards(first, second, attend_w, merge_w, message_gain, message_bias, expand_w, reduce_w, update_gain, update_bias):
    rows = [v.reshape(1, CHAN) for v in (message_gain, message_bias, update_gain, update_bias)]
    operands = (first, second, attend_w, merge_w, rows[0], rows[1], expand_w, reduce_w, rows[2], rows[3])
    vmem = pl.BlockSpec(memory_space=pltpu.VMEM)
    dma = pltpu.SemaphoreType.DMA
    return pl.pallas_call(
        kernel,
        out_shape=jax.ShapeDtypeStruct((2, 4, 64), F32),
        in_specs=[pl.BlockSpec(memory_space=pl.ANY)] * 10,
        out_specs=vmem,
        scratch_shapes=[pltpu.VMEM(v.shape, v.dtype) for v in operands]
        + [
            pltpu.VMEM((2, 2, HEADS, 48, HALF), BF16),
            pltpu.VMEM((CORNER, 48, HALF), BF16),
            pltpu.VMEM((EDGE, 48, HALF), BF16),
            pltpu.VMEM((OWN, 48, HALF), BF16),
            pltpu.VMEM((OTHER, 32, HALF), BF16),
            pltpu.VMEM((8, 16, TILE), BF16),
            pltpu.VMEM((7 * CHUNK, 16), BF16),
            pltpu.VMEM((32, 7 * CHUNK), BF16),
            pltpu.VMEM((2 * CHUNK, TILE), F32),
            pltpu.VMEM((2 * CHUNK, TILE), F32),
            pltpu.VMEM((4, 8, TILE), F32),
            pltpu.VMEM((4, 8, TILE), F32),
            pltpu.VMEM((2 * UNITS, 32, TILE), F32),
            pltpu.VMEM((2 * UNITS, 8, TILE), F32),
            pltpu.VMEM((32, 16, HALF), BF16),
            pltpu.VMEM((2, 2, HEADS, 16, HALF), BF16),
            pltpu.VMEM((GROUP, CELLS, CHAN), BF16),
            pltpu.VMEM((GROUP, CELLS, CHAN), BF16),
            pltpu.VMEM((16, GROUP * CELLS), BF16),
            pltpu.VMEM((4, 16, TILE), F32),
            pltpu.VMEM((GROUP, 8, CELLS), F32),
            pltpu.VMEM((GROUP, 8, CELLS), F32),
        ]
        + [dma] * 8
        + [dma((4,)), dma((4,)), dma, dma, dma((10,)), pltpu.SemaphoreType.REGULAR, dma, dma, dma, dma((4,))],
        compiler_params=pltpu.CompilerParams(
            collective_id=0, has_side_effects=True, vmem_limit_bytes=67000000
        ),
    )(*operands)


def solution(mesh):
    split = P(("pair", "row"), "col", None)
    return jax.shard_map(
        shards,
        mesh=mesh,
        in_specs=(split, split) + (P(),) * 8,
        out_specs=P(None, ("pair", "row"), "col"),
        check_vma=False,
    )
```

```python
import functools
import math

import jax
import jax.numpy as jnp
from jax import lax
from jax.experimental import pallas as pl
from jax.experimental.pallas import tpu as pltpu
from jax.sharding import PartitionSpec as P

HEADS = 8
HEAD_DIM = 16
CHAN = 128
HIDDEN = 1024
NORM_EPSILON = 1e-05
LOG2E = math.log2(math.e)
MESH = pl.DeviceIdType.MESH
F32 = jnp.float32
BF16 = jnp.bfloat16

HALF = 128
TILE = 512
CHUNK = 1024
PIECE = 256
CELLS = 256
CORNER, EDGE, OWN, OTHER = 8, 16, 8, 24
UNITS = 9
ORDER = (0, 1, 3, 2)
GROUP = 8


def nn(a, b):
    return jnp.dot(a, b, preferred_element_type=F32)


def nt(a, b):
    return lax.dot_general(a, b, (((1,), (1,)), ((), ())), preferred_element_type=F32)


def layer_norm(values, gain, bias):
    centre = values - jnp.mean(values, axis=-1, keepdims=True)
    spread = jnp.mean(centre * centre, axis=-1, keepdims=True)
    return centre * lax.rsqrt(spread + NORM_EPSILON) * gain + bias


def erf_gelu(x):
    return 0.5 * x * (1.0 + lax.erf(x * (1.0 / math.sqrt(2.0))))


def unit_tile(n):
    tile = jnp.where(n < 2, n, jnp.where(n < 10, 2 + (n - 2) // 2, 6 + (n - 10) // 4))
    chunk = jnp.where(n < 2, 0, jnp.where(n < 10, 1 + lax.rem(n, 2), 3 + lax.rem(n - 10, 4)))
    return tile, chunk


def kernel(*refs):
    inputs, out, held, refs = refs[:10], refs[10], refs[11:21], refs[21:]
    (first, second, attend_w, merge_w, message_gain, message_bias, expand_w, reduce_w, update_gain, update_bias) = held
    (
    sent, corner, edge, own, other,
    q_all, k_all, v_all, scores_a, scores_b, max_a, max_b, accs, maxes,
    o_all, attended, ref_q, ref_k, where_v, running, partial, parts,
    send_sem, corner_sem, edge_sem, own_sem, other_sem,
    back_send_sem, back_sem, ref_send_sem, q_sem, k_sem, part_send_sem, part_sem, load_sem, core_sem,
    relay_send_sem, relay_sem, q_pass_send_sem, q_pass_sem,
    ) = refs
    loads = [pltpu.make_async_copy(inputs[j], held[j], load_sem.at[j]) for j in range(10)]
    for j in (0, 1, 2, 3, 4, 5, 6, 7, 8, 9):
        loads[j].start()
    pair, r, c = lax.axis_index("pair"), lax.axis_index("row"), lax.axis_index("col")
    place, side = r >> 1, r & 1
    head, frame = place >> 1, place & 1
    own_side = r >> 4
    middle = (r >= 8) & (r < 24)

    barrier = pltpu.get_barrier_semaphore()

    def greet(i, carry):
        to = (r >> 1) * 2 + c + 1 + i & 31
        pl.semaphore_signal(barrier, inc=1, device_id=(pair, (to >> 1) * 2 + (r & 1), to & 1), device_id_type=MESH)
        return carry

    pl.semaphore_signal(barrier, inc=1, device_id=(pair, r ^ 1, c), device_id_type=MESH)
    lax.fori_loop(0, 31, greet, 0, unroll=True)

    for j in (0, 1, 2):
        loads[j].wait()

    weight_t = attend_w[...].T
    for f, source in enumerate((first, second)):
        for half in range(2):
            cells = source[:, 32 * half : 32 * half + 32, :].reshape(HALF, CHAN)
            projected = nt(weight_t, cells)
            queries = projected[:CHAN] * (LOG2E / math.sqrt(HEAD_DIM))
            sent[f, half, :, 0:16, :] = queries.astype(BF16).reshape(HEADS, 16, HALF)
            sent[f, half, :, 16:32, :] = projected[CHAN : 2 * CHAN].astype(BF16).reshape(HEADS, 16, HALF)
            sent[f, half, :, 32:48, :] = projected[2 * CHAN :].astype(BF16).reshape(HEADS, 16, HALF)

    pl.semaphore_wait(barrier, 32)
    pl.semaphore_signal(core_sem, inc=1, device_id=(pair, r ^ 1, c), device_id_type=MESH)
    pl.semaphore_wait(core_sem, 1)

    def transfer(source, target, dest_r, dest_c, s_sem, r_sem, start):
        here = (dest_r == r) & (dest_c == c)

        @pl.when(jnp.logical_not(here))
        def _():
            copy = pltpu.make_async_remote_copy(
                source, target, s_sem, r_sem, device_id=(pair, dest_r, dest_c), device_id_type=MESH
            )
            if start:
                copy.start()
            else:
                copy.wait_send()

        if start:

            @pl.when(here)
            def _():
                pltpu.make_async_copy(source, target, r_sem).start()

    def send_all(start):
        def each(body):
            def step(i, carry):
                d = place + i & 15
                body(d >> 1, d & 1, d)
                return carry

            lax.fori_loop(0, 16, step, 0, unroll=4 if start else 1)

        inner = 1 - c

        @pl.when(middle)
        def _():
            def outer_half(h, f, d):
                transfer(sent.at[f, c, h], edge.at[r - 8], d * 2 + 1 - c, c, send_sem, edge_sem, start)

            def own_half(h, f, d):
                transfer(sent.at[f, inner, h], own.at[r & 7], d * 2 + own_side, c, send_sem, own_sem, start)

            def other_half(h, f, d):
                transfer(
                    sent.at[f, inner, h, 16:48], other.at[r & 7], d * 2 + own_side, 1 - c, send_sem, other_sem, start
                )

            each(outer_half)
            each(own_half)
            each(other_half)

        @pl.when(jnp.logical_not(middle))
        def _():
            def corner_half(h, f, d):
                transfer(sent.at[f, c, h], corner.at[r & 7], d * 2 + own_side, c, send_sem, corner_sem, start)

            def edge_half(h, f, d):
                slot = c * 8 + (r & 7)
                transfer(sent.at[f, inner, h], edge.at[slot], d * 2 + own_side, own_side, send_sem, edge_sem, start)

            each(corner_half)
            each(edge_half)

    send_all(True)

    relays = [
        pltpu.make_async_remote_copy(
            source, target, relay_send_sem, relay_sem, device_id=(pair, r ^ 1, c), device_id_type=MESH
        )
        for source, target in ((own.at[:, 16:48], other.at[8:16]), (other.at[0:8], other.at[16:24]))
    ]

    def arrived(ref, sem):
        pltpu.make_async_copy(ref, ref, sem).wait()

    def take_kv(block, at, first_row):
        k_all[at * HALF : (at + 1) * HALF, :] = block[first_row : first_row + 16, :].astype(F32).T.astype(BF16)
        v_all[0:16, at * HALF : (at + 1) * HALF] = block[first_row + 16 : first_row + 32, :]

    def take_q(block, at):
        q_all[at // 4, :, (at % 4) * HALF : (at % 4 + 1) * HALF] = block[0:16, :]

    def together(score, value, tiles=2, chunk=CHUNK):
        for sub in range(tiles):
            if score:
                scores, top, get_queries, get_keys = score
                queries = get_queries(sub)
                largest = jnp.full((8, TILE), -jnp.inf, F32)
            if value:
                lifted, tops, get_values, put = value
                m = jnp.max(tops[sub], axis=0, keepdims=True)
                acc = None
            for j in range(chunk // PIECE):
                at = slice(sub * chunk + j * PIECE, sub * chunk + (j + 1) * PIECE)
                if score:
                    x = get_keys(sub, j, queries)
                    scores[at, :] = x
                    largest = jnp.maximum(largest, jnp.max(x.reshape(PIECE // 8, 8, TILE), axis=0))
                if value:
                    p = jnp.exp2(lifted[at, :] - m).astype(BF16)
                    product = nn(get_values(sub, j), p)
                    acc = product if acc is None else acc + product
            if score:
                top[sub] = largest
            if value:
                put(sub, m, acc)

    held_scores = ((scores_a, max_a), (scores_b, max_b))

    def attend_score(u, slot):
        def get_queries(sub):
            return q_all[unit_tile(2 * u + sub)[0]]

        def get_scores(sub, j, queries):
            first_key = unit_tile(2 * u + sub)[1] * CHUNK + j * PIECE
            return nn(k_all[pl.ds(pl.multiple_of(first_key, PIECE), PIECE), :], queries)

        return (*held_scores[slot], get_queries, get_scores)

    def attend_value(u, slot):
        def get_values(sub, j):
            first_key = unit_tile(2 * u + sub)[1] * CHUNK + j * PIECE
            return v_all[:, pl.ds(pl.multiple_of(first_key, PIECE), PIECE)]

        def put(sub, m, acc):
            accs[2 * u + sub] = acc
            maxes[2 * u + sub] = jnp.broadcast_to(m, (8, TILE))

        return (*held_scores[slot], get_values, put)

    v_all[16:32, :] = jnp.ones_like(v_all[16:32, :])
    arrived(corner, corner_sem)
    for b in range(CORNER):
        take_kv(corner[b], b, 16)
        take_q(corner[b], b)
    together(attend_score(0, 0), None)
    arrived(edge, edge_sem)
    for b in range(EDGE):
        take_kv(edge[b], 8 + b, 16)
        take_q(edge[b], 8 + b)

    def finish(tile, n, count):
        m = maxes[n, 0:1]
        for j in range(1, count):
            m = jnp.maximum(m, maxes[n + j, 0:1])
        acc = accs[n] * jnp.exp2(maxes[n, 0:1] - m)
        for j in range(1, count):
            acc = acc + accs[n + j] * jnp.exp2(maxes[n + j, 0:1] - m)
        o = (acc[0:16] / acc[16:17]).astype(BF16)
        for b in range(4):
            o_all[4 * tile + b] = o[:, b * HALF : (b + 1) * HALF]

    def give_back(kind, start, first=0, count=8):
        def step(j, carry):
            j = j + first
            if kind == "corner":
                at, to_r, to_c, late = j, side * 24 + j, c, 0
            elif kind == "edge":
                level = side == c
                at = CORNER + j
                to_r = jnp.where(level, side * 24 + (j & 7), 8 + j)
                to_c = jnp.where(level, j >> 3, c)
                late = jnp.where(level, 1, 0)
            else:
                at, to_r, to_c, late = CORNER + EDGE + j, 8 + 8 * side + j, c, 1
            target = attended.at[late, frame, head]
            transfer(o_all.at[at], target, to_r, to_c, back_send_sem, back_sem.at[late], start)
            return carry

        lax.fori_loop(0, count, step, 0, unroll=True if start else 1)

    def two_units(i, carry):
        @pl.when(i == 2)
        def _():
            for b in range(8):
                take_kv(other[b], 32 + b, 0)
            arrived(other.at[8:24], relay_sem)
            for b in range(8, OTHER):
                take_kv(other[b], 32 + b, 0)

        together(attend_score(2 * i + 1, 1), attend_value(2 * i, 0))

        @pl.when(i == 1)
        def _():
            arrived(own, own_sem)
            arrived(other.at[0:8], other_sem)
            for copy in relays:
                copy.start()
            for b in range(OWN):
                take_kv(own[b], 24 + b, 16)
                take_q(own[b], 24 + b)

        @pl.when(i == 2)
        def _():
            for tile in range(2):
                finish(tile, tile, 1)
            give_back("corner", True)
            for tile in range(4):
                finish(2 + tile, 2 + 2 * tile, 2)
            give_back("edge", True, 0, 16)

        together(attend_score(2 * i + 2, 0), attend_value(2 * i + 1, 1))
        return carry

    lax.fori_loop(0, UNITS // 2, two_units, 0)
    finish(6, 10, 4)
    give_back("centre", True, 0, 4)
    together(None, attend_value(UNITS - 1, 0))
    finish(7, 14, 4)
    give_back("centre", True, 4, 4)
    for j in range(3, 10):
        loads[j].wait()

    def refine(late):
        local = pl.ds(pl.multiple_of(32 * (1 - c if late else c), 32), 32)
        cells = jnp.concatenate([source[:, local, :].reshape(HALF, CHAN) for source in (second, first)], axis=0)
        heads = jnp.concatenate(
            [attended[late, f].reshape(CHAN, HALF).astype(F32).T.astype(BF16) for f in (1, 0)], axis=0
        )
        message = layer_norm(nn(heads, merge_w[...]), message_gain[...], message_bias[...]).astype(BF16)
        joined = jnp.concatenate([cells, message], axis=1)
        update = jnp.zeros((2 * HALF, CHAN), F32)
        for j in range(HIDDEN // 256):
            hidden = erf_gelu(nn(joined, expand_w[:, 256 * j : 256 * j + 256])).astype(BF16)
            update = update + nn(hidden, reduce_w[256 * j : 256 * j + 256, :])
        refined = cells.astype(F32) + layer_norm(update, update_gain[...], update_bias[...])
        ref_k[0, late * HALF : (late + 1) * HALF, :] = refined[:HALF].astype(BF16)
        ref_q[0, late * HALF : (late + 1) * HALF, :] = (refined[HALF:] * (LOG2E / math.sqrt(CHAN))).astype(BF16)

    column, line = r & 7, r >> 3

    def spread(kind, late, start):
        half = pl.ds(late * HALF, HALF)

        def step(i, carry):
            if kind == "k":
                to_line, to_c = line + (i >> 1) & 3, c ^ (i & 1)
                at = (4 - (i >> 1) & 3) * 2 + (i & 1)
                ref, sem, to_r = ref_k, k_sem.at[at >> 1], to_line * 8 + column
            else:
                to_c, at = c, (4 - (i >> 1) & 3) * 2 + (i & 1)
                ref, sem, to_r = ref_q, q_pass_sem.at[0] if i == 1 else q_sem.at[at >> 1], line * 8 + ((column >> 1) + (i >> 1) & 3) * 2 + (column & 1 ^ i & 1)
            copy = pltpu.make_async_remote_copy(
                ref.at[0, half], ref.at[at, half], ref_send_sem, sem, device_id=(pair, to_r, to_c), device_id_type=MESH
            )
            if start:
                copy.start()
            else:
                copy.wait_send()
            return carry

        if start:
            for i in (1, 2, 3, 6, 7, 4, 5) if kind == "k" else (1, 2, 6, 4):
                step(i, 0)
        else:
            for i in range(1, GROUP) if kind == "k" else (1, 2, 6, 4):
                step(i, 0)

    for late in range(2):
        arrived(attended.at[late], back_sem.at[late])
        refine(late)
        spread("k", late, True)
        spread("q", late, True)

    at = lax.broadcasted_iota(jnp.int32, (16, CELLS), 1)
    what = lax.broadcasted_iota(jnp.int32, (16, CELLS), 0)
    for k in range(GROUP):
        key_c = c ^ (k % 2)
        key_column = 64 * key_c + 32 * jnp.where(at < HALF, key_c, 1 - key_c) + at % 32
        key_row = 4 * (8 * (line + k // 2 & 3) + column) + (at // 32) % 4
        weigh = jnp.where(what == 0, 1, jnp.where(what == 1, key_column, key_row))
        where_v[:, CELLS * k : CELLS * (k + 1)] = weigh.astype(F32).astype(BF16)

    def corr_score(u, slot):
        def get_queries(sub):
            t = ORDER[sub]
            if u == 0:
                arrived(ref_q.at[2 * t + 1], q_pass_sem.at[t])
            return ref_q[2 * t : 2 * t + 2].reshape(TILE, CHAN)

        def get_scores(sub, j, queries):
            return nt(ref_k[2 * ORDER[u] + j], queries)

        return (*held_scores[slot], get_queries, get_scores)

    def corr_value(u, slot):
        def get_values(sub, j):
            k = 2 * ORDER[u] + j
            return where_v[:, CELLS * k : CELLS * (k + 1)]

        def put(sub, m, acc):
            sums = acc[0:8]
            if u:
                before, m_before = running[sub, 0:8], running[sub, 8:9]
                m_now = jnp.maximum(m, m_before)
                sums = sums * jnp.exp2(m - m_now) + before * jnp.exp2(m_before - m_now)
                m = m_now
            if u < 3:
                running[sub, 0:8] = sums
                running[sub, 8:16] = jnp.broadcast_to(m, (8, TILE))
            else:
                sums = jnp.concatenate([sums[0:7], m], axis=0)
                partial[2 * sub] = sums[:, :CELLS]
                partial[2 * sub + 1] = sums[:, CELLS:]
                hand_in(sub, True)

        return (*held_scores[slot], get_values, put)

    def hand_in(sub, start):
        for i in range(2):
            at = 2 * ORDER[sub] + i
            if at == 0:
                if start:
                    parts[0] = partial[0]
                continue
            to = ((column >> 1) + ORDER[sub] & 3) * 2 + (column & 1 ^ i)
            copy = pltpu.make_async_remote_copy(
                partial.at[2 * sub + i], parts.at[(4 - ORDER[sub]) % 4 * 2 + i], part_send_sem, part_sem,
                device_id=(pair, line * 8 + to, c), device_id_type=MESH,
            )
            if start:
                copy.start()
            else:
                copy.wait_send()

    passes = []
    for t in ORDER[1:]:
        arrived(ref_q.at[2 * t], q_sem.at[t])
        copy = pltpu.make_async_remote_copy(
            ref_q.at[2 * t], ref_q.at[2 * t + 1], q_pass_send_sem, q_pass_sem.at[t],
            device_id=(pair, r ^ 1, c), device_id_type=MESH,
        )
        copy.start()
        passes.append(copy)

    def corr(score, value):
        together(score, value, tiles=4, chunk=2 * CELLS)

    arrived(ref_k.at[1:2], k_sem.at[0])
    corr(corr_score(0, 0), None)
    for u in range(1, 4):
        arrived(ref_k.at[2 * ORDER[u] : 2 * ORDER[u] + 2], k_sem.at[ORDER[u]])
        corr(corr_score(u, u % 2), corr_value(u - 1, (u - 1) % 2))
    corr(None, corr_value(3, 1))
    for copy in relays:
        copy.wait_send()
    send_all(False)
    give_back("corner", False)
    give_back("edge", False, 0, 16)
    give_back("centre", False)
    for late in range(2):
        spread("k", late, False)
        spread("q", late, False)
    for copy in passes:
        copy.wait_send()
    for sub in range(4):
        hand_in(sub, False)
    arrived(parts.at[1:8], part_sem)

    m = jnp.max(parts[:, 7:8, :], axis=0)
    total = jnp.zeros((8, CELLS), F32)
    for j in range(GROUP):
        total = total + parts[j] * jnp.exp2(parts[j, 7:8, :] - m)
    lane = lax.broadcasted_iota(jnp.int32, (1, CELLS), 1)
    own_column = (64 * c + 32 * jnp.where(lane < HALF, c, 1 - c) + lane % 32).astype(F32)
    own_row = (4 * r + (lane // 32) % 4).astype(F32)
    flows = (
        (total[1:2] / total[0:1] - own_column) * (2.0 / 128),
        (total[2:3] / total[0:1] - own_row) * (2.0 / 128),
    )
    for which in range(2):
        for i in range(4):
            early, late = (flows[which][:, at : at + 32] for at in (32 * i, HALF + 32 * i))
            out[which, i : i + 1, 0:32] = jnp.where(c == 0, early, late)
            out[which, i : i + 1, 32:64] = jnp.where(c == 0, late, early)


def shards(first, second, attend_w, merge_w, message_gain, message_bias, expand_w, reduce_w, update_gain, update_bias):
    rows = [v.reshape(1, CHAN) for v in (message_gain, message_bias, update_gain, update_bias)]
    operands = (first, second, attend_w, merge_w, rows[0], rows[1], expand_w, reduce_w, rows[2], rows[3])
    vmem = pl.BlockSpec(memory_space=pltpu.VMEM)
    dma = pltpu.SemaphoreType.DMA
    return pl.pallas_call(
        kernel,
        out_shape=jax.ShapeDtypeStruct((2, 4, 64), F32),
        in_specs=[pl.BlockSpec(memory_space=pl.ANY)] * 10,
        out_specs=vmem,
        scratch_shapes=[pltpu.VMEM(v.shape, v.dtype) for v in operands]
        + [
            pltpu.VMEM((2, 2, HEADS, 48, HALF), BF16),
            pltpu.VMEM((CORNER, 48, HALF), BF16),
            pltpu.VMEM((EDGE, 48, HALF), BF16),
            pltpu.VMEM((OWN, 48, HALF), BF16),
            pltpu.VMEM((OTHER, 32, HALF), BF16),
            pltpu.VMEM((8, 16, TILE), BF16),
            pltpu.VMEM((7 * CHUNK, 16), BF16),
            pltpu.VMEM((32, 7 * CHUNK), BF16),
            pltpu.VMEM((2 * CHUNK, TILE), F32),
            pltpu.VMEM((2 * CHUNK, TILE), F32),
            pltpu.VMEM((4, 8, TILE), F32),
            pltpu.VMEM((4, 8, TILE), F32),
            pltpu.VMEM((2 * UNITS, 32, TILE), F32),
            pltpu.VMEM((2 * UNITS, 8, TILE), F32),
            pltpu.VMEM((32, 16, HALF), BF16),
            pltpu.VMEM((2, 2, HEADS, 16, HALF), BF16),
            pltpu.VMEM((GROUP, CELLS, CHAN), BF16),
            pltpu.VMEM((GROUP, CELLS, CHAN), BF16),
            pltpu.VMEM((16, GROUP * CELLS), BF16),
            pltpu.VMEM((4, 16, TILE), F32),
            pltpu.VMEM((GROUP, 8, CELLS), F32),
            pltpu.VMEM((GROUP, 8, CELLS), F32),
        ]
        + [dma] * 6
        + [dma((2,)), dma]
        + [dma((4,)), dma((4,)), dma, dma, dma((10,)), pltpu.SemaphoreType.REGULAR, dma, dma, dma, dma((4,))],
        compiler_params=pltpu.CompilerParams(
            collective_id=0, has_side_effects=True, vmem_limit_bytes=67000000
        ),
    )(*operands)


def solution(mesh):
    split = P(("pair", "row"), "col", None)
    return jax.shard_map(
        shards,
        mesh=mesh,
        in_specs=(split, split) + (P(),) * 8,
        out_specs=P(None, ("pair", "row"), "col"),
        check_vma=False,
    )
```

```python
import functools
import math

import jax
import jax.numpy as jnp
from jax import lax
from jax.experimental import pallas as pl
from jax.experimental.pallas import tpu as pltpu
from jax.sharding import PartitionSpec as P

HEADS = 8
HEAD_DIM = 16
CHAN = 128
HIDDEN = 1024
NORM_EPSILON = 1e-05
LOG2E = math.log2(math.e)
MESH = pl.DeviceIdType.MESH
F32 = jnp.float32
BF16 = jnp.bfloat16

HALF = 128
TILE = 512
CHUNK = 1024
PIECE = 256
CORNER, EDGE, OWN, OTHER = 8, 16, 8, 24
UNITS = 9
ORDER = (0, 1, 3, 2)
GROUP = 8


def nn(a, b):
    return jnp.dot(a, b, preferred_element_type=F32)


def nt(a, b):
    return lax.dot_general(a, b, (((1,), (1,)), ((), ())), preferred_element_type=F32)


def layer_norm(values, gain, bias):
    centre = values - jnp.mean(values, axis=-1, keepdims=True)
    spread = jnp.mean(centre * centre, axis=-1, keepdims=True)
    return centre * lax.rsqrt(spread + NORM_EPSILON) * gain + bias


def erf_gelu(x):
    return 0.5 * x * (1.0 + lax.erf(x * (1.0 / math.sqrt(2.0))))


def unit_tile(n):
    tile = jnp.where(n < 2, n, jnp.where(n < 10, 2 + (n - 2) // 2, 6 + (n - 10) // 4))
    chunk = jnp.where(n < 2, 0, jnp.where(n < 10, 1 + lax.rem(n, 2), 3 + lax.rem(n - 10, 4)))
    return tile, chunk


def kernel(*refs):
    inputs, out, held, refs = refs[:10], refs[10], refs[11:21], refs[21:]
    (first, second, attend_w, merge_w, message_gain, message_bias, expand_w, reduce_w, update_gain, update_bias) = held
    (
    sent, corner, edge, own, other,
    q_all, k_all, v_all, scores_a, scores_b, max_a, max_b, accs, maxes,
    o_all, attended, ref_q, ref_k, where_v, running, partial, parts,
    send_sem, corner_sem, edge_sem, own_sem, other_sem,
    back_send_sem, back_sem, ref_send_sem, q_sem, k_sem, part_send_sem, part_sem, load_sem, core_sem,
    relay_send_sem, relay_sem, q_pass_send_sem, q_pass_sem,
    ) = refs
    loads = [pltpu.make_async_copy(inputs[j], held[j], load_sem.at[j]) for j in range(10)]
    for j in (0, 1, 2, 3, 4, 5, 6, 7, 8, 9):
        loads[j].start()
    pair, r, c = lax.axis_index("pair"), lax.axis_index("row"), lax.axis_index("col")
    place, side = r >> 1, r & 1
    head, frame = place >> 1, place & 1
    own_side = r >> 4
    middle = (r >= 8) & (r < 24)

    barrier = pltpu.get_barrier_semaphore()

    def greet(i, carry):
        to = (r >> 1) * 2 + c + 1 + i & 31
        pl.semaphore_signal(barrier, inc=1, device_id=(pair, (to >> 1) * 2 + (r & 1), to & 1), device_id_type=MESH)
        return carry

    pl.semaphore_signal(barrier, inc=1, device_id=(pair, r ^ 1, c), device_id_type=MESH)
    lax.fori_loop(0, 31, greet, 0, unroll=True)

    for j in (0, 1, 2):
        loads[j].wait()

    weight_t = attend_w[...].T
    for f, source in enumerate((first, second)):
        for half in range(2):
            cells = source[:, 32 * half : 32 * half + 32, :].reshape(HALF, CHAN)
            projected = nt(weight_t, cells)
            queries = projected[:CHAN] * (LOG2E / math.sqrt(HEAD_DIM))
            sent[f, half, :, 0:16, :] = queries.astype(BF16).reshape(HEADS, 16, HALF)
            sent[f, half, :, 16:32, :] = projected[CHAN : 2 * CHAN].astype(BF16).reshape(HEADS, 16, HALF)
            sent[f, half, :, 32:48, :] = projected[2 * CHAN :].astype(BF16).reshape(HEADS, 16, HALF)

    pl.semaphore_wait(barrier, 32)
    pl.semaphore_signal(core_sem, inc=1, device_id=(pair, r ^ 1, c), device_id_type=MESH)
    pl.semaphore_wait(core_sem, 1)

    def transfer(source, target, dest_r, dest_c, s_sem, r_sem, start):
        here = (dest_r == r) & (dest_c == c)

        @pl.when(jnp.logical_not(here))
        def _():
            copy = pltpu.make_async_remote_copy(
                source, target, s_sem, r_sem, device_id=(pair, dest_r, dest_c), device_id_type=MESH
            )
            if start:
                copy.start()
            else:
                copy.wait_send()

        if start:

            @pl.when(here)
            def _():
                pltpu.make_async_copy(source, target, r_sem).start()

    def send_all(start):
        def each(body):
            def step(i, carry):
                d = place + i & 15
                body(d >> 1, d & 1, d)
                return carry

            lax.fori_loop(0, 16, step, 0, unroll=4 if start else 1)

        inner = 1 - c

        @pl.when(middle)
        def _():
            def outer_half(h, f, d):
                transfer(sent.at[f, c, h], edge.at[r - 8], d * 2 + 1 - c, c, send_sem, edge_sem, start)

            def own_half(h, f, d):
                transfer(sent.at[f, inner, h], own.at[r & 7], d * 2 + own_side, c, send_sem, own_sem, start)

            def other_half(h, f, d):
                transfer(
                    sent.at[f, inner, h, 16:48], other.at[r & 7], d * 2 + own_side, 1 - c, send_sem, other_sem, start
                )

            each(outer_half)
            each(own_half)
            each(other_half)

        @pl.when(jnp.logical_not(middle))
        def _():
            def corner_half(h, f, d):
                transfer(sent.at[f, c, h], corner.at[r & 7], d * 2 + own_side, c, send_sem, corner_sem, start)

            def edge_half(h, f, d):
                slot = c * 8 + (r & 7)
                transfer(sent.at[f, inner, h], edge.at[slot], d * 2 + own_side, own_side, send_sem, edge_sem, start)

            each(corner_half)
            each(edge_half)

    send_all(True)

    relays = [
        pltpu.make_async_remote_copy(
            source, target, relay_send_sem, relay_sem, device_id=(pair, r ^ 1, c), device_id_type=MESH
        )
        for source, target in ((own.at[:, 16:48], other.at[8:16]), (other.at[0:8], other.at[16:24]))
    ]

    def arrived(ref, sem):
        pltpu.make_async_copy(ref, ref, sem).wait()

    def take_kv(block, at, first_row):
        k_all[at * HALF : (at + 1) * HALF, :] = block[first_row : first_row + 16, :].astype(F32).T.astype(BF16)
        v_all[0:16, at * HALF : (at + 1) * HALF] = block[first_row + 16 : first_row + 32, :]

    def take_q(block, at):
        q_all[at // 4, :, (at % 4) * HALF : (at % 4 + 1) * HALF] = block[0:16, :]

    def together(score, value, tiles=2, chunk=CHUNK):
        for sub in range(tiles):
            if score:
                scores, top, get_queries, get_keys = score
                queries = get_queries(sub)
                largest = jnp.full((8, TILE), -jnp.inf, F32)
            if value:
                lifted, tops, get_values, put = value
                m = jnp.max(tops[sub], axis=0, keepdims=True)
                acc = None
            for j in range(chunk // PIECE):
                at = slice(sub * chunk + j * PIECE, sub * chunk + (j + 1) * PIECE)
                if score:
                    x = get_keys(sub, j, queries)
                    scores[at, :] = x
                    largest = jnp.maximum(largest, jnp.max(x.reshape(PIECE // 8, 8, TILE), axis=0))
                if value:
                    p = jnp.exp2(lifted[at, :] - m).astype(BF16)
                    product = nn(get_values(sub, j), p)
                    acc = product if acc is None else acc + product
            if score:
                top[sub] = largest
            if value:
                put(sub, m, acc)

    held_scores = ((scores_a, max_a), (scores_b, max_b))

    def attend_score(u, slot):
        def get_queries(sub):
            return q_all[unit_tile(2 * u + sub)[0]]

        def get_scores(sub, j, queries):
            first_key = unit_tile(2 * u + sub)[1] * CHUNK + j * PIECE
            return nn(k_all[pl.ds(pl.multiple_of(first_key, PIECE), PIECE), :], queries)

        return (*held_scores[slot], get_queries, get_scores)

    def attend_value(u, slot):
        def get_values(sub, j):
            first_key = unit_tile(2 * u + sub)[1] * CHUNK + j * PIECE
            return v_all[:, pl.ds(pl.multiple_of(first_key, PIECE), PIECE)]

        def put(sub, m, acc):
            accs[2 * u + sub] = acc
            maxes[2 * u + sub] = jnp.broadcast_to(m, (8, TILE))

        return (*held_scores[slot], get_values, put)

    v_all[16:32, :] = jnp.ones_like(v_all[16:32, :])
    arrived(corner, corner_sem)
    for b in range(CORNER):
        take_kv(corner[b], b, 16)
        take_q(corner[b], b)
    together(attend_score(0, 0), None)
    arrived(edge, edge_sem)
    for b in range(EDGE):
        take_kv(edge[b], 8 + b, 16)
        take_q(edge[b], 8 + b)

    def finish(tile, n, count):
        m = maxes[n, 0:1]
        for j in range(1, count):
            m = jnp.maximum(m, maxes[n + j, 0:1])
        acc = accs[n] * jnp.exp2(maxes[n, 0:1] - m)
        for j in range(1, count):
            acc = acc + accs[n + j] * jnp.exp2(maxes[n + j, 0:1] - m)
        o = (acc[0:16] / acc[16:17]).astype(BF16)
        for b in range(4):
            o_all[4 * tile + b] = o[:, b * HALF : (b + 1) * HALF]

    def give_back(kind, start, first=0, count=8):
        def step(j, carry):
            j = j + first
            if kind == "corner":
                at, to_r, to_c, late = j, side * 24 + j, c, 0
            elif kind == "edge":
                level = side == c
                at = CORNER + j
                to_r = jnp.where(level, side * 24 + (j & 7), 8 + j)
                to_c = jnp.where(level, j >> 3, c)
                late = jnp.where(level, 1, 0)
            else:
                at, to_r, to_c, late = CORNER + EDGE + j, 8 + 8 * side + j, c, 1
            target = attended.at[late, frame, head]
            transfer(o_all.at[at], target, to_r, to_c, back_send_sem, back_sem.at[late], start)
            return carry

        lax.fori_loop(0, count, step, 0, unroll=True if start else 1)

    def two_units(i, carry):
        @pl.when(i == 2)
        def _():
            for b in range(8):
                take_kv(other[b], 32 + b, 0)
            arrived(other.at[8:24], relay_sem)
            for b in range(8, OTHER):
                take_kv(other[b], 32 + b, 0)

        together(attend_score(2 * i + 1, 1), attend_value(2 * i, 0))

        @pl.when(i == 1)
        def _():
            arrived(own, own_sem)
            arrived(other.at[0:8], other_sem)
            for copy in relays:
                copy.start()
            for b in range(OWN):
                take_kv(own[b], 24 + b, 16)
                take_q(own[b], 24 + b)

        @pl.when(i == 2)
        def _():
            for tile in range(2):
                finish(tile, tile, 1)
            give_back("corner", True)
            for tile in range(4):
                finish(2 + tile, 2 + 2 * tile, 2)
            give_back("edge", True, 0, 16)

        together(attend_score(2 * i + 2, 0), attend_value(2 * i + 1, 1))
        return carry

    lax.fori_loop(0, UNITS // 2, two_units, 0)
    finish(6, 10, 4)
    give_back("centre", True, 0, 4)
    together(None, attend_value(UNITS - 1, 0))
    finish(7, 14, 4)
    give_back("centre", True, 4, 4)
    for j in range(3, 10):
        loads[j].wait()

    def refine(late):
        local = pl.ds(pl.multiple_of(32 * (1 - c if late else c), 32), 32)
        cells = jnp.concatenate([source[:, local, :].reshape(HALF, CHAN) for source in (second, first)], axis=0)
        heads = jnp.concatenate(
            [attended[late, f].reshape(CHAN, HALF).astype(F32).T.astype(BF16) for f in (1, 0)], axis=0
        )
        message = layer_norm(nn(heads, merge_w[...]), message_gain[...], message_bias[...]).astype(BF16)
        joined = jnp.concatenate([cells, message], axis=1)
        update = jnp.zeros((2 * HALF, CHAN), F32)
        for j in range(HIDDEN // 256):
            hidden = erf_gelu(nn(joined, expand_w[:, 256 * j : 256 * j + 256])).astype(BF16)
            update = update + nn(hidden, reduce_w[256 * j : 256 * j + 256, :])
        refined = cells.astype(F32) + layer_norm(update, update_gain[...], update_bias[...])
        ref_k[late, 0] = refined[:HALF].astype(BF16)
        ref_q[late, 0] = (refined[HALF:] * (LOG2E / math.sqrt(CHAN))).astype(BF16)

    column, line = r & 7, r >> 3

    def spread(kind, late, start):
        def step(i, carry):
            if kind == "k":
                to_line, to_c = line + (i >> 1) & 3, c ^ (i & 1)
                at = (4 - (i >> 1) & 3) * 2 + (i & 1)
                ref, sem, to_r = ref_k, k_sem.at[late], to_line * 8 + column
            else:
                to_c, at = c, (4 - (i >> 1) & 3) * 2 + (i & 1)
                ref, sem, to_r = ref_q, q_pass_sem.at[late] if i == 1 else q_sem.at[4 * late + (at >> 1)], line * 8 + ((column >> 1) + (i >> 1) & 3) * 2 + (column & 1 ^ i & 1)
            copy = pltpu.make_async_remote_copy(
                ref.at[late, 0], ref.at[late, at], ref_send_sem, sem, device_id=(pair, to_r, to_c), device_id_type=MESH
            )
            if start:
                copy.start()
            else:
                copy.wait_send()
            return carry

        if start:
            for i in (1, 2, 3, 6, 7, 4, 5) if kind == "k" else (1, 2, 6, 4):
                step(i, 0)
        else:
            for i in range(1, GROUP) if kind == "k" else (1, 2, 6, 4):
                step(i, 0)

    for late in range(2):
        arrived(attended.at[late], back_sem.at[late])
        refine(late)
        spread("k", late, True)
        spread("q", late, True)

    at = lax.broadcasted_iota(jnp.int32, (16, HALF), 1)
    what = lax.broadcasted_iota(jnp.int32, (16, HALF), 0)
    for late in range(2):
        for k in range(GROUP):
            key_c = c ^ (k % 2)
            key_column = 64 * key_c + 32 * (1 - key_c if late else key_c) + at % 32
            key_row = 4 * (8 * (line + k // 2 & 3) + column) + at // 32
            weigh = jnp.where(what == 0, 1, jnp.where(what == 1, key_column, key_row))
            where_v[late, :, HALF * k : HALF * (k + 1)] = weigh.astype(F32).astype(BF16)

    def corr_score(late_k, late_q, slot):
        def get_queries(sub):
            return ref_q[late_q, 4 * sub : 4 * sub + 4].reshape(TILE, CHAN)

        def get_scores(sub, j, queries):
            return nt(ref_k[late_k, 2 * j : 2 * j + 2].reshape(PIECE, CHAN), queries)

        return (*held_scores[slot], get_queries, get_scores)

    def corr_value(late_k, late_q, slot):
        def get_values(sub, j):
            return where_v[late_k, :, PIECE * j : PIECE * (j + 1)]

        def put(sub, m, acc):
            sums, at = acc[0:8], 2 * late_q + sub
            if not late_k:
                running[at, 0:8] = sums
                running[at, 8:16] = jnp.broadcast_to(m, (8, TILE))
                return
            before, m_before = running[at, 0:8], running[at, 8:9]
            m_now = jnp.maximum(m, m_before)
            sums = sums * jnp.exp2(m - m_now) + before * jnp.exp2(m_before - m_now)
            sums = jnp.concatenate([sums[0:7], m_now], axis=0)
            for j in range(4):
                partial[late_q, 4 * sub + j] = sums[:, HALF * j : HALF * (j + 1)]
            hand_in(late_q, sub, True)

        return (*held_scores[slot], get_values, put)

    def hand_in(late, sub, start):
        for at in range(4 * sub, 4 * sub + 4):
            t, i = at // 2, at % 2
            if at == 0:
                if start:
                    parts[late, 0] = partial[late, 0]
                continue
            to = ((column >> 1) + t & 3) * 2 + (column & 1 ^ i)
            copy = pltpu.make_async_remote_copy(
                partial.at[late, at], parts.at[late, (4 - t) % 4 * 2 + i], part_send_sem, part_sem.at[late],
                device_id=(pair, line * 8 + to, c), device_id_type=MESH,
            )
            if start:
                copy.start()
            else:
                copy.wait_send()

    passes = []

    def pass_on(late):
        for t in ORDER[1:]:
            arrived(ref_q.at[late, 2 * t], q_sem.at[4 * late + t])
            copy = pltpu.make_async_remote_copy(
                ref_q.at[late, 2 * t], ref_q.at[late, 2 * t + 1], q_pass_send_sem, q_pass_sem.at[late],
                device_id=(pair, r ^ 1, c), device_id_type=MESH,
            )
            copy.start()
            passes.append(copy)

    pass_on(0)
    arrived(ref_k.at[0, 1:8], k_sem.at[0])
    arrived(ref_q.at[0, 0:4], q_pass_sem.at[0])
    together(corr_score(0, 0, 0), None)
    together(None, corr_value(0, 0, 0))
    pass_on(1)
    arrived(ref_q.at[1, 0:4], q_pass_sem.at[1])
    together(corr_score(0, 1, 1), None)
    arrived(ref_k.at[1, 1:8], k_sem.at[1])
    together(corr_score(1, 0, 0), corr_value(0, 1, 1))
    together(corr_score(1, 1, 1), corr_value(1, 0, 0))
    together(None, corr_value(1, 1, 1))
    for copy in relays:
        copy.wait_send()
    send_all(False)
    give_back("corner", False)
    give_back("edge", False, 0, 16)
    give_back("centre", False)
    for copy in passes:
        copy.wait_send()
    for late in range(2):
        spread("k", late, False)
        spread("q", late, False)
        hand_in(late, 0, False)
        hand_in(late, 1, False)

    lane = lax.broadcasted_iota(jnp.int32, (1, HALF), 1)
    flows = []
    for late in range(2):
        arrived(parts.at[late, 1:8], part_sem.at[late])
        m = jnp.max(parts[late, :, 7:8, :], axis=0)
        total = jnp.zeros((8, HALF), F32)
        for j in range(GROUP):
            total = total + parts[late, j] * jnp.exp2(parts[late, j, 7:8, :] - m)
        own_column = (64 * c + 32 * (1 - c if late else c) + lane % 32).astype(F32)
        own_row = (4 * r + lane // 32).astype(F32)
        flows.append(
            (
                (total[1:2] / total[0:1] - own_column) * (2.0 / 128),
                (total[2:3] / total[0:1] - own_row) * (2.0 / 128),
            )
        )
    for which in range(2):
        for i in range(4):
            early, late = (flow[which][:, 32 * i : 32 * i + 32] for flow in flows)
            out[which, i : i + 1, 0:32] = jnp.where(c == 0, early, late)
            out[which, i : i + 1, 32:64] = jnp.where(c == 0, late, early)


def shards(first, second, attend_w, merge_w, message_gain, message_bias, expand_w, reduce_w, update_gain, update_bias):
    rows = [v.reshape(1, CHAN) for v in (message_gain, message_bias, update_gain, update_bias)]
    operands = (first, second, attend_w, merge_w, rows[0], rows[1], expand_w, reduce_w, rows[2], rows[3])
    vmem = pl.BlockSpec(memory_space=pltpu.VMEM)
    dma = pltpu.SemaphoreType.DMA
    return pl.pallas_call(
        kernel,
        out_shape=jax.ShapeDtypeStruct((2, 4, 64), F32),
        in_specs=[pl.BlockSpec(memory_space=pl.ANY)] * 10,
        out_specs=vmem,
        scratch_shapes=[pltpu.VMEM(v.shape, v.dtype) for v in operands]
        + [
            pltpu.VMEM((2, 2, HEADS, 48, HALF), BF16),
            pltpu.VMEM((CORNER, 48, HALF), BF16),
            pltpu.VMEM((EDGE, 48, HALF), BF16),
            pltpu.VMEM((OWN, 48, HALF), BF16),
            pltpu.VMEM((OTHER, 32, HALF), BF16),
            pltpu.VMEM((8, 16, TILE), BF16),
            pltpu.VMEM((7 * CHUNK, 16), BF16),
            pltpu.VMEM((32, 7 * CHUNK), BF16),
            pltpu.VMEM((2 * CHUNK, TILE), F32),
            pltpu.VMEM((2 * CHUNK, TILE), F32),
            pltpu.VMEM((4, 8, TILE), F32),
            pltpu.VMEM((4, 8, TILE), F32),
            pltpu.VMEM((2 * UNITS, 32, TILE), F32),
            pltpu.VMEM((2 * UNITS, 8, TILE), F32),
            pltpu.VMEM((32, 16, HALF), BF16),
            pltpu.VMEM((2, 2, HEADS, 16, HALF), BF16),
            pltpu.VMEM((2, GROUP, HALF, CHAN), BF16),
            pltpu.VMEM((2, GROUP, HALF, CHAN), BF16),
            pltpu.VMEM((2, 16, GROUP * HALF), BF16),
            pltpu.VMEM((4, 16, TILE), F32),
            pltpu.VMEM((2, GROUP, 8, HALF), F32),
            pltpu.VMEM((2, GROUP, 8, HALF), F32),
        ]
        + [dma] * 6
        + [dma((2,)), dma]
        + [dma((8,)), dma((2,)), dma, dma((2,)), dma((10,)), pltpu.SemaphoreType.REGULAR, dma, dma, dma, dma((2,))],
        compiler_params=pltpu.CompilerParams(
            collective_id=0, has_side_effects=True, vmem_limit_bytes=67000000
        ),
    )(*operands)


def solution(mesh):
    split = P(("pair", "row"), "col", None)
    return jax.shard_map(
        shards,
        mesh=mesh,
        in_specs=(split, split) + (P(),) * 8,
        out_specs=P(None, ("pair", "row"), "col"),
        check_vma=False,
    )
```

```python
import functools
import math

import jax
import jax.numpy as jnp
from jax import lax
from jax.experimental import pallas as pl
from jax.experimental.pallas import tpu as pltpu
from jax.sharding import PartitionSpec as P

HEADS = 8
HEAD_DIM = 16
CHAN = 128
HIDDEN = 1024
NORM_EPSILON = 1e-05
LOG2E = math.log2(math.e)
MESH = pl.DeviceIdType.MESH
F32 = jnp.float32
BF16 = jnp.bfloat16

HALF = 128
TILE = 512
CHUNK = 1024
PIECE = 256
CORNER, EDGE, OWN, OTHER = 8, 16, 8, 24
UNITS = 9
ORDER = (0, 1, 3, 2)
GROUP = 8


HOPS = (0, 1, 2, 1)
OFFSETS = sorted(((dx, dy) for dx in range(4) for dy in range(4)), key=lambda d: -HOPS[d[0]] - HOPS[d[1]])


def nn(a, b):
    return jnp.dot(a, b, preferred_element_type=F32)


def nt(a, b):
    return lax.dot_general(a, b, (((1,), (1,)), ((), ())), preferred_element_type=F32)


def layer_norm(values, gain, bias):
    centre = values - jnp.mean(values, axis=-1, keepdims=True)
    spread = jnp.mean(centre * centre, axis=-1, keepdims=True)
    return centre * lax.rsqrt(spread + NORM_EPSILON) * gain + bias


def erf_gelu(x):
    return 0.5 * x * (1.0 + lax.erf(x * (1.0 / math.sqrt(2.0))))


def unit_tile(n):
    tile = jnp.where(n < 2, n, jnp.where(n < 10, 2 + (n - 2) // 2, 6 + (n - 10) // 4))
    chunk = jnp.where(n < 2, 0, jnp.where(n < 10, 1 + lax.rem(n, 2), 3 + lax.rem(n - 10, 4)))
    return tile, chunk


def kernel(*refs):
    inputs, out, held, refs = refs[:10], refs[10], refs[11:21], refs[21:]
    (first, second, attend_w, merge_w, message_gain, message_bias, expand_w, reduce_w, update_gain, update_bias) = held
    (
    sent, corner, edge, own, other,
    q_all, k_all, v_all, scores_a, scores_b, max_a, max_b, accs, maxes,
    o_all, attended, ref_q, ref_k, where_v, running, partial, parts,
    send_sem, corner_sem, edge_sem, own_sem, other_sem,
    back_send_sem, back_sem, ref_send_sem, q_sem, k_sem, part_send_sem, part_sem, load_sem, core_sem,
    relay_send_sem, relay_sem, q_pass_send_sem, q_pass_sem,
    ) = refs
    loads = [pltpu.make_async_copy(inputs[j], held[j], load_sem.at[j]) for j in range(10)]
    for j in (0, 1, 2, 3, 4, 5, 6, 7, 8, 9):
        loads[j].start()
    pair, r, c = lax.axis_index("pair"), lax.axis_index("row"), lax.axis_index("col")
    place, side = r >> 1, r & 1
    head, frame = place >> 1, place & 1
    own_side = r >> 4
    middle = (r >= 8) & (r < 24)

    barrier = pltpu.get_barrier_semaphore()

    for dx, dy in OFFSETS:
        to = ((r >> 3) + dx & 3) * 8 + ((r >> 1) + dy & 3) * 2 + (r & 1)
        for to_c in (1 - c, c) if dx or dy else (1 - c,):
            pl.semaphore_signal(barrier, inc=1, device_id=(pair, to, to_c), device_id_type=MESH)
    pl.semaphore_signal(barrier, inc=1, device_id=(pair, r ^ 1, c), device_id_type=MESH)

    for j in (0, 1, 2):
        loads[j].wait()

    weight_t = attend_w[...].T
    for f, source in enumerate((first, second)):
        for half in range(2):
            cells = source[:, 32 * half : 32 * half + 32, :].reshape(HALF, CHAN)
            projected = nt(weight_t, cells)
            queries = projected[:CHAN] * (LOG2E / math.sqrt(HEAD_DIM))
            sent[f, half, :, 0:16, :] = queries.astype(BF16).reshape(HEADS, 16, HALF)
            sent[f, half, :, 16:32, :] = projected[CHAN : 2 * CHAN].astype(BF16).reshape(HEADS, 16, HALF)
            sent[f, half, :, 32:48, :] = projected[2 * CHAN :].astype(BF16).reshape(HEADS, 16, HALF)

    pl.semaphore_wait(barrier, 32)
    pl.semaphore_signal(core_sem, inc=1, device_id=(pair, r ^ 1, c), device_id_type=MESH)
    pl.semaphore_wait(core_sem, 1)

    def transfer(source, target, dest_r, dest_c, s_sem, r_sem, start, near):
        if not near:
            copy = pltpu.make_async_remote_copy(
                source, target, s_sem, r_sem, device_id=(pair, dest_r, dest_c), device_id_type=MESH
            )
            if start:
                copy.start()
            else:
                copy.wait_send()
            return

        here = (dest_r == r) & (dest_c == c)

        @pl.when(jnp.logical_not(here))
        def _():
            copy = pltpu.make_async_remote_copy(
                source, target, s_sem, r_sem, device_id=(pair, dest_r, dest_c), device_id_type=MESH
            )
            if start:
                copy.start()
            else:
                copy.wait_send()

        if start:

            @pl.when(here)
            def _():
                pltpu.make_async_copy(source, target, r_sem).start()

    def send_all(start):
        def each(body):
            for dx, dy in OFFSETS:
                d = ((r >> 3) + dx & 3) * 4 + ((r >> 1) + dy & 3)
                body(d >> 1, d & 1, d, not (dx or dy))

        inner = 1 - c

        @pl.when(middle)
        def _():
            def outer_half(h, f, d, near):
                transfer(sent.at[f, c, h], edge.at[r - 8], d * 2 + 1 - c, c, send_sem, edge_sem, start, near)

            def own_half(h, f, d, near):
                transfer(sent.at[f, inner, h], own.at[r & 7], d * 2 + own_side, c, send_sem, own_sem, start, near)

            def other_half(h, f, d, near):
                transfer(
                    sent.at[f, inner, h, 16:48], other.at[r & 7], d * 2 + own_side, 1 - c, send_sem, other_sem, start, False
                )

            each(outer_half)
            each(own_half)
            each(other_half)

        @pl.when(jnp.logical_not(middle))
        def _():
            def corner_half(h, f, d, near):
                transfer(sent.at[f, c, h], corner.at[r & 7], d * 2 + own_side, c, send_sem, corner_sem, start, near)

            def edge_half(h, f, d, near):
                slot = c * 8 + (r & 7)
                transfer(sent.at[f, inner, h], edge.at[slot], d * 2 + own_side, own_side, send_sem, edge_sem, start, near)

            each(corner_half)
            each(edge_half)

    send_all(True)

    relays = [
        pltpu.make_async_remote_copy(
            source, target, relay_send_sem, relay_sem, device_id=(pair, r ^ 1, c), device_id_type=MESH
        )
        for source, target in ((own.at[:, 16:48], other.at[8:16]), (other.at[0:8], other.at[16:24]))
    ]

    def arrived(ref, sem):
        pltpu.make_async_copy(ref, ref, sem).wait()

    def take_kv(block, at, first_row):
        k_all[at * HALF : (at + 1) * HALF, :] = block[first_row : first_row + 16, :].astype(F32).T.astype(BF16)
        v_all[0:16, at * HALF : (at + 1) * HALF] = block[first_row + 16 : first_row + 32, :]

    def take_q(block, at):
        q_all[at // 4, :, (at % 4) * HALF : (at % 4 + 1) * HALF] = block[0:16, :]

    def together(score, value, tiles=2, chunk=CHUNK):
        for sub in range(tiles):
            if score:
                scores, top, get_queries, get_keys = score
                queries = get_queries(sub)
                largest = jnp.full((8, TILE), -jnp.inf, F32)
            if value:
                lifted, tops, get_values, put = value
                m = jnp.max(tops[sub], axis=0, keepdims=True)
                acc = None
            for j in range(chunk // PIECE):
                at = slice(sub * chunk + j * PIECE, sub * chunk + (j + 1) * PIECE)
                if score:
                    x = get_keys(sub, j, queries)
                    scores[at, :] = x
                    largest = jnp.maximum(largest, jnp.max(x.reshape(PIECE // 8, 8, TILE), axis=0))
                if value:
                    p = jnp.exp2(lifted[at, :] - m).astype(BF16)
                    product = nn(get_values(sub, j), p)
                    acc = product if acc is None else acc + product
            if score:
                top[sub] = largest
            if value:
                put(sub, m, acc)

    held_scores = ((scores_a, max_a), (scores_b, max_b))

    def attend_score(u, slot):
        def get_queries(sub):
            return q_all[unit_tile(2 * u + sub)[0]]

        def get_scores(sub, j, queries):
            first_key = unit_tile(2 * u + sub)[1] * CHUNK + j * PIECE
            return nn(k_all[pl.ds(pl.multiple_of(first_key, PIECE), PIECE), :], queries)

        return (*held_scores[slot], get_queries, get_scores)

    def attend_value(u, slot):
        def get_values(sub, j):
            first_key = unit_tile(2 * u + sub)[1] * CHUNK + j * PIECE
            return v_all[:, pl.ds(pl.multiple_of(first_key, PIECE), PIECE)]

        def put(sub, m, acc):
            accs[2 * u + sub] = acc
            maxes[2 * u + sub] = jnp.broadcast_to(m, (8, TILE))

        return (*held_scores[slot], get_values, put)

    v_all[16:32, :] = jnp.ones_like(v_all[16:32, :])
    arrived(corner, corner_sem)
    for b in range(CORNER):
        take_kv(corner[b], b, 16)
        take_q(corner[b], b)
    together(attend_score(0, 0), None)
    arrived(edge, edge_sem)
    for b in range(EDGE):
        take_kv(edge[b], 8 + b, 16)
        take_q(edge[b], 8 + b)

    def finish(tile, n, count):
        m = maxes[n, 0:1]
        for j in range(1, count):
            m = jnp.maximum(m, maxes[n + j, 0:1])
        acc = accs[n] * jnp.exp2(maxes[n, 0:1] - m)
        for j in range(1, count):
            acc = acc + accs[n + j] * jnp.exp2(maxes[n + j, 0:1] - m)
        o = (acc[0:16] / acc[16:17]).astype(BF16)
        for b in range(4):
            o_all[4 * tile + b] = o[:, b * HALF : (b + 1) * HALF]

    def give_back(kind, start, first=0, count=8):
        def step(j, carry):
            j = j + first
            if kind == "corner":
                at, to_r, to_c, late = j, side * 24 + j, c, 0
            elif kind == "edge":
                level = side == c
                at = CORNER + j
                to_r = jnp.where(level, side * 24 + (j & 7), 8 + j)
                to_c = jnp.where(level, j >> 3, c)
                late = jnp.where(level, 1, 0)
            else:
                at, to_r, to_c, late = CORNER + EDGE + j, 8 + 8 * side + j, c, 1
            target = attended.at[late, frame, head]
            transfer(o_all.at[at], target, to_r, to_c, back_send_sem, back_sem.at[late], start, True)
            return carry

        lax.fori_loop(0, count, step, 0, unroll=True if start else 1)

    def two_units(i, carry):
        @pl.when(i == 2)
        def _():
            for b in range(8):
                take_kv(other[b], 32 + b, 0)
            arrived(other.at[8:24], relay_sem)
            for b in range(8, OTHER):
                take_kv(other[b], 32 + b, 0)

        together(attend_score(2 * i + 1, 1), attend_value(2 * i, 0))

        @pl.when(i == 1)
        def _():
            arrived(own, own_sem)
            arrived(other.at[0:8], other_sem)
            for copy in relays:
                copy.start()
            for b in range(OWN):
                take_kv(own[b], 24 + b, 16)
                take_q(own[b], 24 + b)

        @pl.when(i == 2)
        def _():
            for tile in range(2):
                finish(tile, tile, 1)
            give_back("corner", True)
            for tile in range(4):
                finish(2 + tile, 2 + 2 * tile, 2)
            give_back("edge", True, 0, 16)

        together(attend_score(2 * i + 2, 0), attend_value(2 * i + 1, 1))
        return carry

    lax.fori_loop(0, UNITS // 2, two_units, 0)
    finish(6, 10, 4)
    give_back("centre", True, 0, 4)
    together(None, attend_value(UNITS - 1, 0))
    finish(7, 14, 4)
    give_back("centre", True, 4, 4)
    for j in range(3, 10):
        loads[j].wait()

    def refine(late):
        local = pl.ds(pl.multiple_of(32 * (1 - c if late else c), 32), 32)
        cells = jnp.concatenate([source[:, local, :].reshape(HALF, CHAN) for source in (second, first)], axis=0)
        heads = jnp.concatenate(
            [attended[late, f].reshape(CHAN, HALF).astype(F32).T.astype(BF16) for f in (1, 0)], axis=0
        )
        message = layer_norm(nn(heads, merge_w[...]), message_gain[...], message_bias[...]).astype(BF16)
        joined = jnp.concatenate([cells, message], axis=1)
        update = jnp.zeros((2 * HALF, CHAN), F32)
        for j in range(HIDDEN // 256):
            hidden = erf_gelu(nn(joined, expand_w[:, 256 * j : 256 * j + 256])).astype(BF16)
            update = update + nn(hidden, reduce_w[256 * j : 256 * j + 256, :])
        refined = cells.astype(F32) + layer_norm(update, update_gain[...], update_bias[...])
        ref_k[late, 0] = refined[:HALF].astype(BF16)
        ref_q[late, 0] = (refined[HALF:] * (LOG2E / math.sqrt(CHAN))).astype(BF16)

    column, line = r & 7, r >> 3

    def spread(kind, late, start):
        def step(i, carry):
            if kind == "k":
                to_line, to_c = line + (i >> 1) & 3, c ^ (i & 1)
                at = (4 - (i >> 1) & 3) * 2 + (i & 1)
                ref, sem, to_r = ref_k, k_sem.at[late], to_line * 8 + column
            else:
                to_c, at = c, (4 - (i >> 1) & 3) * 2 + (i & 1)
                ref, sem, to_r = ref_q, q_pass_sem.at[late] if i == 1 else q_sem.at[4 * late + (at >> 1)], line * 8 + ((column >> 1) + (i >> 1) & 3) * 2 + (column & 1 ^ i & 1)
            copy = pltpu.make_async_remote_copy(
                ref.at[late, 0], ref.at[late, at], ref_send_sem, sem, device_id=(pair, to_r, to_c), device_id_type=MESH
            )
            if start:
                copy.start()
            else:
                copy.wait_send()
            return carry

        if start:
            for i in (1, 2, 3, 6, 7, 4, 5) if kind == "k" else (1, 2, 6, 4):
                step(i, 0)
        else:
            for i in range(1, GROUP) if kind == "k" else (1, 2, 6, 4):
                step(i, 0)

    for late in range(2):
        arrived(attended.at[late], back_sem.at[late])
        refine(late)
        spread("q", late, True)
        spread("k", late, True)

    at = lax.broadcasted_iota(jnp.int32, (16, HALF), 1)
    what = lax.broadcasted_iota(jnp.int32, (16, HALF), 0)
    for late in range(2):
        for k in range(GROUP):
            key_c = c ^ (k % 2)
            key_column = 64 * key_c + 32 * (1 - key_c if late else key_c) + at % 32
            key_row = 4 * (8 * (line + k // 2 & 3) + column) + at // 32
            weigh = jnp.where(what == 0, 1, jnp.where(what == 1, key_column, key_row))
            where_v[late, :, HALF * k : HALF * (k + 1)] = weigh.astype(F32).astype(BF16)

    def corr_score(late_k, late_q, slot):
        def get_queries(sub):
            return ref_q[late_q, 4 * sub : 4 * sub + 4].reshape(TILE, CHAN)

        def get_scores(sub, j, queries):
            return nt(ref_k[late_k, 2 * j : 2 * j + 2].reshape(PIECE, CHAN), queries)

        return (*held_scores[slot], get_queries, get_scores)

    def corr_value(late_k, late_q, slot):
        def get_values(sub, j):
            return where_v[late_k, :, PIECE * j : PIECE * (j + 1)]

        def put(sub, m, acc):
            sums, at = acc[0:8], 2 * late_q + sub
            if not late_k:
                running[at, 0:8] = sums
                running[at, 8:16] = jnp.broadcast_to(m, (8, TILE))
                return
            before, m_before = running[at, 0:8], running[at, 8:9]
            m_now = jnp.maximum(m, m_before)
            sums = sums * jnp.exp2(m - m_now) + before * jnp.exp2(m_before - m_now)
            sums = jnp.concatenate([sums[0:7], m_now], axis=0)
            for j in range(4):
                partial[late_q, 4 * sub + j] = sums[:, HALF * j : HALF * (j + 1)]
            hand_in(late_q, sub, True)

        return (*held_scores[slot], get_values, put)

    def hand_in(late, sub, start):
        for at in range(4 * sub, 4 * sub + 4):
            t, i = at // 2, at % 2
            if at == 0:
                if start:
                    parts[late, 0] = partial[late, 0]
                continue
            to = ((column >> 1) + t & 3) * 2 + (column & 1 ^ i)
            copy = pltpu.make_async_remote_copy(
                partial.at[late, at], parts.at[late, (4 - t) % 4 * 2 + i], part_send_sem, part_sem.at[late],
                device_id=(pair, line * 8 + to, c), device_id_type=MESH,
            )
            if start:
                copy.start()
            else:
                copy.wait_send()

    passes = []

    def pass_on(late):
        for t in ORDER[1:]:
            arrived(ref_q.at[late, 2 * t], q_sem.at[4 * late + t])
            copy = pltpu.make_async_remote_copy(
                ref_q.at[late, 2 * t], ref_q.at[late, 2 * t + 1], q_pass_send_sem, q_pass_sem.at[late],
                device_id=(pair, r ^ 1, c), device_id_type=MESH,
            )
            copy.start()
            passes.append(copy)

    pass_on(0)
    arrived(ref_k.at[0, 1:8], k_sem.at[0])
    arrived(ref_q.at[0, 0:4], q_pass_sem.at[0])
    together(corr_score(0, 0, 0), None)
    pass_on(1)
    together(None, corr_value(0, 0, 0))
    arrived(ref_q.at[1, 0:4], q_pass_sem.at[1])
    together(corr_score(0, 1, 1), None)
    arrived(ref_k.at[1, 1:8], k_sem.at[1])
    together(corr_score(1, 0, 0), corr_value(0, 1, 1))
    together(corr_score(1, 1, 1), corr_value(1, 0, 0))
    together(None, corr_value(1, 1, 1))
    for copy in relays:
        copy.wait_send()
    send_all(False)
    give_back("corner", False)
    give_back("edge", False, 0, 16)
    give_back("centre", False)
    for copy in passes:
        copy.wait_send()
    for late in range(2):
        spread("k", late, False)
        spread("q", late, False)
        hand_in(late, 0, False)
        hand_in(late, 1, False)

    lane = lax.broadcasted_iota(jnp.int32, (1, HALF), 1)
    flows = []
    for late in range(2):
        arrived(parts.at[late, 1:8], part_sem.at[late])
        m = jnp.max(parts[late, :, 7:8, :], axis=0)
        total = jnp.zeros((8, HALF), F32)
        for j in range(GROUP):
            total = total + parts[late, j] * jnp.exp2(parts[late, j, 7:8, :] - m)
        own_column = (64 * c + 32 * (1 - c if late else c) + lane % 32).astype(F32)
        own_row = (4 * r + lane // 32).astype(F32)
        flows.append(
            (
                (total[1:2] / total[0:1] - own_column) * (2.0 / 128),
                (total[2:3] / total[0:1] - own_row) * (2.0 / 128),
            )
        )
    for which in range(2):
        for i in range(4):
            early, late = (flow[which][:, 32 * i : 32 * i + 32] for flow in flows)
            out[which, i : i + 1, 0:32] = jnp.where(c == 0, early, late)
            out[which, i : i + 1, 32:64] = jnp.where(c == 0, late, early)


def shards(first, second, attend_w, merge_w, message_gain, message_bias, expand_w, reduce_w, update_gain, update_bias):
    rows = [v.reshape(1, CHAN) for v in (message_gain, message_bias, update_gain, update_bias)]
    operands = (first, second, attend_w, merge_w, rows[0], rows[1], expand_w, reduce_w, rows[2], rows[3])
    vmem = pl.BlockSpec(memory_space=pltpu.VMEM)
    dma = pltpu.SemaphoreType.DMA
    return pl.pallas_call(
        kernel,
        out_shape=jax.ShapeDtypeStruct((2, 4, 64), F32),
        in_specs=[pl.BlockSpec(memory_space=pl.ANY)] * 10,
        out_specs=vmem,
        scratch_shapes=[pltpu.VMEM(v.shape, v.dtype) for v in operands]
        + [
            pltpu.VMEM((2, 2, HEADS, 48, HALF), BF16),
            pltpu.VMEM((CORNER, 48, HALF), BF16),
            pltpu.VMEM((EDGE, 48, HALF), BF16),
            pltpu.VMEM((OWN, 48, HALF), BF16),
            pltpu.VMEM((OTHER, 32, HALF), BF16),
            pltpu.VMEM((8, 16, TILE), BF16),
            pltpu.VMEM((7 * CHUNK, 16), BF16),
            pltpu.VMEM((32, 7 * CHUNK), BF16),
            pltpu.VMEM((2 * CHUNK, TILE), F32),
            pltpu.VMEM((2 * CHUNK, TILE), F32),
            pltpu.VMEM((4, 8, TILE), F32),
            pltpu.VMEM((4, 8, TILE), F32),
            pltpu.VMEM((2 * UNITS, 32, TILE), F32),
            pltpu.VMEM((2 * UNITS, 8, TILE), F32),
            pltpu.VMEM((32, 16, HALF), BF16),
            pltpu.VMEM((2, 2, HEADS, 16, HALF), BF16),
            pltpu.VMEM((2, GROUP, HALF, CHAN), BF16),
            pltpu.VMEM((2, GROUP, HALF, CHAN), BF16),
            pltpu.VMEM((2, 16, GROUP * HALF), BF16),
            pltpu.VMEM((4, 16, TILE), F32),
            pltpu.VMEM((2, GROUP, 8, HALF), F32),
            pltpu.VMEM((2, GROUP, 8, HALF), F32),
        ]
        + [dma] * 6
        + [dma((2,)), dma]
        + [dma((8,)), dma((2,)), dma, dma((2,)), dma((10,)), pltpu.SemaphoreType.REGULAR, dma, dma, dma, dma((2,))],
        compiler_params=pltpu.CompilerParams(
            collective_id=0, has_side_effects=True, vmem_limit_bytes=56522000
        ),
    )(*operands)


def solution(mesh):
    split = P(("pair", "row"), "col", None)
    return jax.shard_map(
        shards,
        mesh=mesh,
        in_specs=(split, split) + (P(),) * 8,
        out_specs=P(None, ("pair", "row"), "col"),
        check_vma=False,
    )
```

```python
import functools
import math

import jax
import jax.numpy as jnp
from jax import lax
from jax.experimental import pallas as pl
from jax.experimental.pallas import tpu as pltpu
from jax.sharding import PartitionSpec as P

HEADS = 8
HEAD_DIM = 16
CHAN = 128
HIDDEN = 1024
NORM_EPSILON = 1e-05
LOG2E = math.log2(math.e)
MESH = pl.DeviceIdType.MESH
F32 = jnp.float32
BF16 = jnp.bfloat16

HALF = 128
TILE = 512
CHUNK = 1024
PIECE = 256
CORNER, EDGE, OWN, OTHER = 8, 16, 8, 24
UNITS = 9
ORDER = (0, 1, 3, 2)
GROUP = 8


HOPS = (0, 1, 2, 1)
OFFSETS = sorted(((dx, dy) for dx in range(4) for dy in range(4)), key=lambda d: -HOPS[d[0]] - HOPS[d[1]])


def nn(a, b):
    return jnp.dot(a, b, preferred_element_type=F32)


def nt(a, b):
    return lax.dot_general(a, b, (((1,), (1,)), ((), ())), preferred_element_type=F32)


def layer_norm(values, gain, bias):
    centre = values - jnp.mean(values, axis=-1, keepdims=True)
    spread = jnp.mean(centre * centre, axis=-1, keepdims=True)
    return centre * lax.rsqrt(spread + NORM_EPSILON) * gain + bias


def erf_gelu(x):
    return 0.5 * x * (1.0 + lax.erf(x * (1.0 / math.sqrt(2.0))))


def unit_tile(n):
    tile = jnp.where(n < 2, n, jnp.where(n < 10, 2 + (n - 2) // 2, 6 + (n - 10) // 4))
    chunk = jnp.where(n < 2, 0, jnp.where(n < 10, 1 + lax.rem(n, 2), 3 + lax.rem(n - 10, 4)))
    return tile, chunk


def kernel(*refs):
    inputs, out, held, refs = refs[:10], refs[10], refs[11:21], refs[21:]
    (first, second, attend_w, merge_w, message_gain, message_bias, expand_w, reduce_w, update_gain, update_bias) = held
    (
    sent, corner, edge, own, other,
    q_all, k_all, v_all, scores_a, scores_b, max_a, max_b, accs, maxes,
    o_all, attended, ref_q, ref_k, where_v, running, partial, parts,
    send_sem, corner_sem, edge_sem, own_sem, other_sem,
    back_send_sem, back_sem, ref_send_sem, q_sem, k_sem, part_send_sem, part_sem, load_sem, core_sem,
    relay_send_sem, relay_sem, q_pass_send_sem, q_pass_sem,
    ) = refs
    loads = [pltpu.make_async_copy(inputs[j], held[j], load_sem.at[j]) for j in range(10)]
    for j in (0, 1, 2):
        loads[j].start()
    pair, r, c = lax.axis_index("pair"), lax.axis_index("row"), lax.axis_index("col")
    place, side = r >> 1, r & 1
    head, frame = place >> 1, place & 1
    own_side = r >> 4
    middle = (r >= 8) & (r < 24)

    barrier = pltpu.get_barrier_semaphore()

    for dx, dy in OFFSETS:
        to = ((r >> 3) + dx & 3) * 8 + ((r >> 1) + dy & 3) * 2 + (r & 1)
        for to_c in (1 - c, c) if dx or dy else (1 - c,):
            pl.semaphore_signal(barrier, inc=1, device_id=(pair, to, to_c), device_id_type=MESH)
    pl.semaphore_signal(barrier, inc=1, device_id=(pair, r ^ 1, c), device_id_type=MESH)

    for j in range(3, 10):
        loads[j].start()
    for j in (0, 1, 2):
        loads[j].wait()

    weight_t = attend_w[...].T
    for f, source in enumerate((first, second)):
        for half in range(2):
            cells = source[:, 32 * half : 32 * half + 32, :].reshape(HALF, CHAN)
            projected = nt(weight_t, cells)
            queries = projected[:CHAN] * (LOG2E / math.sqrt(HEAD_DIM))
            sent[f, half, :, 0:16, :] = queries.astype(BF16).reshape(HEADS, 16, HALF)
            sent[f, half, :, 16:32, :] = projected[CHAN : 2 * CHAN].astype(BF16).reshape(HEADS, 16, HALF)
            sent[f, half, :, 32:48, :] = projected[2 * CHAN :].astype(BF16).reshape(HEADS, 16, HALF)

    pl.semaphore_wait(barrier, 32)
    pl.semaphore_signal(core_sem, inc=1, device_id=(pair, r ^ 1, c), device_id_type=MESH)
    pl.semaphore_wait(core_sem, 1)

    def transfer(source, target, dest_r, dest_c, s_sem, r_sem, start, near):
        if not near:
            copy = pltpu.make_async_remote_copy(
                source, target, s_sem, r_sem, device_id=(pair, dest_r, dest_c), device_id_type=MESH
            )
            if start:
                copy.start()
            else:
                copy.wait_send()
            return

        here = (dest_r == r) & (dest_c == c)

        @pl.when(jnp.logical_not(here))
        def _():
            copy = pltpu.make_async_remote_copy(
                source, target, s_sem, r_sem, device_id=(pair, dest_r, dest_c), device_id_type=MESH
            )
            if start:
                copy.start()
            else:
                copy.wait_send()

        if start:

            @pl.when(here)
            def _():
                pltpu.make_async_copy(source, target, r_sem).start()

    def send_all(start):
        def each(body):
            for dx, dy in OFFSETS:
                d = ((r >> 3) + dx & 3) * 4 + ((r >> 1) + dy & 3)
                body(d >> 1, d & 1, d, not (dx or dy))

        inner = 1 - c

        @pl.when(middle)
        def _():
            def outer_half(h, f, d, near):
                transfer(sent.at[f, c, h], edge.at[r - 8], d * 2 + 1 - c, c, send_sem, edge_sem, start, near)

            def own_half(h, f, d, near):
                transfer(sent.at[f, inner, h], own.at[r & 7], d * 2 + own_side, c, send_sem, own_sem, start, near)

            def other_half(h, f, d, near):
                transfer(
                    sent.at[f, inner, h, 16:48], other.at[r & 7], d * 2 + own_side, 1 - c, send_sem, other_sem, start, False
                )

            each(outer_half)
            each(own_half)
            each(other_half)

        @pl.when(jnp.logical_not(middle))
        def _():
            def corner_half(h, f, d, near):
                transfer(sent.at[f, c, h], corner.at[r & 7], d * 2 + own_side, c, send_sem, corner_sem, start, near)

            def edge_half(h, f, d, near):
                slot = c * 8 + (r & 7)
                transfer(sent.at[f, inner, h], edge.at[slot], d * 2 + own_side, own_side, send_sem, edge_sem, start, near)

            each(corner_half)
            each(edge_half)

    send_all(True)

    relays = [
        pltpu.make_async_remote_copy(
            source, target, relay_send_sem, relay_sem, device_id=(pair, r ^ 1, c), device_id_type=MESH
        )
        for source, target in ((own.at[:, 16:48], other.at[8:16]), (other.at[0:8], other.at[16:24]))
    ]

    def arrived(ref, sem):
        pltpu.make_async_copy(ref, ref, sem).wait()

    def take_kv(block, at, first_row):
        k_all[at * HALF : (at + 1) * HALF, :] = block[first_row : first_row + 16, :].astype(F32).T.astype(BF16)
        v_all[0:16, at * HALF : (at + 1) * HALF] = block[first_row + 16 : first_row + 32, :]

    def take_q(block, at):
        q_all[at // 4, :, (at % 4) * HALF : (at % 4 + 1) * HALF] = block[0:16, :]

    def together(score, value, tiles=2, chunk=CHUNK):
        for sub in range(tiles):
            if score:
                scores, top, get_queries, get_keys = score
                queries = get_queries(sub)
                largest = jnp.full((8, TILE), -jnp.inf, F32)
            if value:
                lifted, tops, get_values, put = value
                m = jnp.max(tops[sub], axis=0, keepdims=True)
                acc = None
            for j in range(chunk // PIECE):
                at = slice(sub * chunk + j * PIECE, sub * chunk + (j + 1) * PIECE)
                if score:
                    x = get_keys(sub, j, queries)
                    scores[at, :] = x
                    largest = jnp.maximum(largest, jnp.max(x.reshape(PIECE // 8, 8, TILE), axis=0))
                if value:
                    p = jnp.exp2(lifted[at, :] - m).astype(BF16)
                    product = nn(get_values(sub, j), p)
                    acc = product if acc is None else acc + product
            if score:
                top[sub] = largest
            if value:
                put(sub, m, acc)

    held_scores = ((scores_a, max_a), (scores_b, max_b))

    def attend_score(u, slot):
        def get_queries(sub):
            return q_all[unit_tile(2 * u + sub)[0]]

        def get_scores(sub, j, queries):
            first_key = unit_tile(2 * u + sub)[1] * CHUNK + j * PIECE
            return nn(k_all[pl.ds(pl.multiple_of(first_key, PIECE), PIECE), :], queries)

        return (*held_scores[slot], get_queries, get_scores)

    def attend_value(u, slot):
        def get_values(sub, j):
            first_key = unit_tile(2 * u + sub)[1] * CHUNK + j * PIECE
            return v_all[:, pl.ds(pl.multiple_of(first_key, PIECE), PIECE)]

        def put(sub, m, acc):
            accs[2 * u + sub] = acc
            maxes[2 * u + sub] = jnp.broadcast_to(m, (8, TILE))

        return (*held_scores[slot], get_values, put)

    v_all[16:32, :] = jnp.ones_like(v_all[16:32, :])
    arrived(corner, corner_sem)
    for b in range(CORNER):
        take_kv(corner[b], b, 16)
        take_q(corner[b], b)
    together(attend_score(0, 0), None)
    arrived(edge, edge_sem)
    for b in range(EDGE):
        take_kv(edge[b], 8 + b, 16)
        take_q(edge[b], 8 + b)

    def finish(tile, n, count):
        m = maxes[n, 0:1]
        for j in range(1, count):
            m = jnp.maximum(m, maxes[n + j, 0:1])
        acc = accs[n] * jnp.exp2(maxes[n, 0:1] - m)
        for j in range(1, count):
            acc = acc + accs[n + j] * jnp.exp2(maxes[n + j, 0:1] - m)
        o = (acc[0:16] / acc[16:17]).astype(BF16)
        for b in range(4):
            o_all[4 * tile + b] = o[:, b * HALF : (b + 1) * HALF]

    def give_back(kind, start, first=0, count=8):
        def step(j, carry):
            j = j + first
            if kind == "corner":
                at, to_r, to_c, late = j, side * 24 + j, c, 0
            elif kind == "edge":
                level = side == c
                at = CORNER + j
                to_r = jnp.where(level, side * 24 + (j & 7), 8 + j)
                to_c = jnp.where(level, j >> 3, c)
                late = jnp.where(level, 1, 0)
            else:
                at, to_r, to_c, late = CORNER + EDGE + j, 8 + 8 * side + j, c, 1
            target = attended.at[late, frame, head]
            transfer(o_all.at[at], target, to_r, to_c, back_send_sem, back_sem.at[late], start, True)
            return carry

        lax.fori_loop(0, count, step, 0, unroll=True if start else 1)

    def two_units(i, carry):
        @pl.when(i == 2)
        def _():
            for b in range(8):
                take_kv(other[b], 32 + b, 0)
            arrived(other.at[8:24], relay_sem)
            for b in range(8, OTHER):
                take_kv(other[b], 32 + b, 0)

        together(attend_score(2 * i + 1, 1), attend_value(2 * i, 0))

        @pl.when(i == 1)
        def _():
            arrived(own, own_sem)
            arrived(other.at[0:8], other_sem)
            for copy in relays:
                copy.start()
            for b in range(OWN):
                take_kv(own[b], 24 + b, 16)
                take_q(own[b], 24 + b)

        @pl.when(i == 2)
        def _():
            for tile in range(2):
                finish(tile, tile, 1)
            give_back("corner", True)
            for tile in range(4):
                finish(2 + tile, 2 + 2 * tile, 2)
            give_back("edge", True, 0, 16)

        together(attend_score(2 * i + 2, 0), attend_value(2 * i + 1, 1))
        return carry

    lax.fori_loop(0, UNITS // 2, two_units, 0)
    finish(6, 10, 4)
    give_back("centre", True, 0, 4)
    together(None, attend_value(UNITS - 1, 0))
    finish(7, 14, 4)
    give_back("centre", True, 4, 4)
    for j in range(3, 10):
        loads[j].wait()

    def refine(late):
        local = pl.ds(pl.multiple_of(32 * (1 - c if late else c), 32), 32)
        cells = jnp.concatenate([source[:, local, :].reshape(HALF, CHAN) for source in (second, first)], axis=0)
        heads = jnp.concatenate(
            [attended[late, f].reshape(CHAN, HALF).astype(F32).T.astype(BF16) for f in (1, 0)], axis=0
        )
        message = layer_norm(nn(heads, merge_w[...]), message_gain[...], message_bias[...]).astype(BF16)
        joined = jnp.concatenate([cells, message], axis=1)
        update = jnp.zeros((2 * HALF, CHAN), F32)
        for j in range(HIDDEN // 256):
            hidden = erf_gelu(nn(joined, expand_w[:, 256 * j : 256 * j + 256])).astype(BF16)
            update = update + nn(hidden, reduce_w[256 * j : 256 * j + 256, :])
        refined = cells.astype(F32) + layer_norm(update, update_gain[...], update_bias[...])
        ref_k[late, 0] = refined[:HALF].astype(BF16)
        ref_q[late, 0] = (refined[HALF:] * (LOG2E / math.sqrt(CHAN))).astype(BF16)

    column, line = r & 7, r >> 3

    def spread(kind, late, start):
        def step(i, carry):
            if kind == "k":
                to_line, to_c = line + (i >> 1) & 3, c ^ (i & 1)
                at = (4 - (i >> 1) & 3) * 2 + (i & 1)
                ref, sem, to_r = ref_k, k_sem.at[late], to_line * 8 + column
            else:
                to_c, at = c, (4 - (i >> 1) & 3) * 2 + (i & 1)
                ref, sem, to_r = ref_q, q_pass_sem.at[late] if i == 1 else q_sem.at[4 * late + (at >> 1)], line * 8 + ((column >> 1) + (i >> 1) & 3) * 2 + (column & 1 ^ i & 1)
            copy = pltpu.make_async_remote_copy(
                ref.at[late, 0], ref.at[late, at], ref_send_sem, sem, device_id=(pair, to_r, to_c), device_id_type=MESH
            )
            if start:
                copy.start()
            else:
                copy.wait_send()
            return carry

        if start:
            for i in (1, 2, 3, 6, 7, 4, 5) if kind == "k" else (1, 2, 6, 4):
                step(i, 0)
        else:
            for i in range(1, GROUP) if kind == "k" else (1, 2, 6, 4):
                step(i, 0)

    for late in range(2):
        arrived(attended.at[late], back_sem.at[late])
        refine(late)
        spread("q", late, True)
        spread("k", late, True)

    at = lax.broadcasted_iota(jnp.int32, (16, HALF), 1)
    what = lax.broadcasted_iota(jnp.int32, (16, HALF), 0)
    for late in range(2):
        for k in range(GROUP):
            key_c = c ^ (k % 2)
            key_column = 64 * key_c + 32 * (1 - key_c if late else key_c) + at % 32
            key_row = 4 * (8 * (line + k // 2 & 3) + column) + at // 32
            weigh = jnp.where(what == 0, 1, jnp.where(what == 1, key_column, key_row))
            where_v[late, :, HALF * k : HALF * (k + 1)] = weigh.astype(F32).astype(BF16)

    def corr_score(late_k, late_q, slot):
        def get_queries(sub):
            return ref_q[late_q, 4 * sub : 4 * sub + 4].reshape(TILE, CHAN)

        def get_scores(sub, j, queries):
            return nt(ref_k[late_k, 2 * j : 2 * j + 2].reshape(PIECE, CHAN), queries)

        return (*held_scores[slot], get_queries, get_scores)

    def corr_value(late_k, late_q, slot):
        def get_values(sub, j):
            return where_v[late_k, :, PIECE * j : PIECE * (j + 1)]

        def put(sub, m, acc):
            sums, at = acc[0:8], 2 * late_q + sub
            if not late_k:
                running[at, 0:8] = sums
                running[at, 8:16] = jnp.broadcast_to(m, (8, TILE))
                return
            before, m_before = running[at, 0:8], running[at, 8:9]
            m_now = jnp.maximum(m, m_before)
            sums = sums * jnp.exp2(m - m_now) + before * jnp.exp2(m_before - m_now)
            sums = jnp.concatenate([sums[0:7], m_now], axis=0)
            for j in range(4):
                partial[late_q, 4 * sub + j] = sums[:, HALF * j : HALF * (j + 1)]
            hand_in(late_q, sub, True)

        return (*held_scores[slot], get_values, put)

    def hand_in(late, sub, start):
        for at in range(4 * sub, 4 * sub + 4):
            t, i = at // 2, at % 2
            if at == 0:
                if start:
                    parts[late, 0] = partial[late, 0]
                continue
            to = ((column >> 1) + t & 3) * 2 + (column & 1 ^ i)
            copy = pltpu.make_async_remote_copy(
                partial.at[late, at], parts.at[late, (4 - t) % 4 * 2 + i], part_send_sem, part_sem.at[late],
                device_id=(pair, line * 8 + to, c), device_id_type=MESH,
            )
            if start:
                copy.start()
            else:
                copy.wait_send()

    passes = []

    def pass_on(late):
        for t in ORDER[1:]:
            arrived(ref_q.at[late, 2 * t], q_sem.at[4 * late + t])
            copy = pltpu.make_async_remote_copy(
                ref_q.at[late, 2 * t], ref_q.at[late, 2 * t + 1], q_pass_send_sem, q_pass_sem.at[late],
                device_id=(pair, r ^ 1, c), device_id_type=MESH,
            )
            copy.start()
            passes.append(copy)

    pass_on(0)
    arrived(ref_k.at[0, 1:8], k_sem.at[0])
    arrived(ref_q.at[0, 0:4], q_pass_sem.at[0])
    together(corr_score(0, 0, 0), None)
    pass_on(1)
    together(None, corr_value(0, 0, 0))
    arrived(ref_q.at[1, 0:4], q_pass_sem.at[1])
    together(corr_score(0, 1, 1), None)
    arrived(ref_k.at[1, 1:8], k_sem.at[1])
    together(corr_score(1, 0, 0), corr_value(0, 1, 1))
    together(corr_score(1, 1, 1), corr_value(1, 0, 0))
    together(None, corr_value(1, 1, 1))
    for copy in relays:
        copy.wait_send()
    send_all(False)
    give_back("corner", False)
    give_back("edge", False, 0, 16)
    give_back("centre", False)
    for copy in passes:
        copy.wait_send()
    for late in range(2):
        spread("k", late, False)
        spread("q", late, False)
        hand_in(late, 0, False)
        hand_in(late, 1, False)

    lane = lax.broadcasted_iota(jnp.int32, (1, HALF), 1)
    flows = []
    for late in range(2):
        arrived(parts.at[late, 1:8], part_sem.at[late])
        m = jnp.max(parts[late, :, 7:8, :], axis=0)
        total = jnp.zeros((8, HALF), F32)
        for j in range(GROUP):
            total = total + parts[late, j] * jnp.exp2(parts[late, j, 7:8, :] - m)
        own_column = (64 * c + 32 * (1 - c if late else c) + lane % 32).astype(F32)
        own_row = (4 * r + lane // 32).astype(F32)
        flows.append(
            (
                (total[1:2] / total[0:1] - own_column) * (2.0 / 128),
                (total[2:3] / total[0:1] - own_row) * (2.0 / 128),
            )
        )
    for which in range(2):
        for i in range(4):
            early, late = (flow[which][:, 32 * i : 32 * i + 32] for flow in flows)
            out[which, i : i + 1, 0:32] = jnp.where(c == 0, early, late)
            out[which, i : i + 1, 32:64] = jnp.where(c == 0, late, early)


def shards(first, second, attend_w, merge_w, message_gain, message_bias, expand_w, reduce_w, update_gain, update_bias):
    rows = [v.reshape(1, CHAN) for v in (message_gain, message_bias, update_gain, update_bias)]
    operands = (first, second, attend_w, merge_w, rows[0], rows[1], expand_w, reduce_w, rows[2], rows[3])
    vmem = pl.BlockSpec(memory_space=pltpu.VMEM)
    dma = pltpu.SemaphoreType.DMA
    return pl.pallas_call(
        kernel,
        out_shape=jax.ShapeDtypeStruct((2, 4, 64), F32),
        in_specs=[pl.BlockSpec(memory_space=pl.ANY)] * 10,
        out_specs=vmem,
        scratch_shapes=[pltpu.VMEM(v.shape, v.dtype) for v in operands]
        + [
            pltpu.VMEM((2, 2, HEADS, 48, HALF), BF16),
            pltpu.VMEM((CORNER, 48, HALF), BF16),
            pltpu.VMEM((EDGE, 48, HALF), BF16),
            pltpu.VMEM((OWN, 48, HALF), BF16),
            pltpu.VMEM((OTHER, 32, HALF), BF16),
            pltpu.VMEM((8, 16, TILE), BF16),
            pltpu.VMEM((7 * CHUNK, 16), BF16),
            pltpu.VMEM((32, 7 * CHUNK), BF16),
            pltpu.VMEM((2 * CHUNK, TILE), F32),
            pltpu.VMEM((2 * CHUNK, TILE), F32),
            pltpu.VMEM((4, 8, TILE), F32),
            pltpu.VMEM((4, 8, TILE), F32),
            pltpu.VMEM((2 * UNITS, 32, TILE), F32),
            pltpu.VMEM((2 * UNITS, 8, TILE), F32),
            pltpu.VMEM((32, 16, HALF), BF16),
            pltpu.VMEM((2, 2, HEADS, 16, HALF), BF16),
            pltpu.VMEM((2, GROUP, HALF, CHAN), BF16),
            pltpu.VMEM((2, GROUP, HALF, CHAN), BF16),
            pltpu.VMEM((2, 16, GROUP * HALF), BF16),
            pltpu.VMEM((4, 16, TILE), F32),
            pltpu.VMEM((2, GROUP, 8, HALF), F32),
            pltpu.VMEM((2, GROUP, 8, HALF), F32),
        ]
        + [dma] * 6
        + [dma((2,)), dma]
        + [dma((8,)), dma((2,)), dma, dma((2,)), dma((10,)), pltpu.SemaphoreType.REGULAR, dma, dma, dma, dma((2,))],
        compiler_params=pltpu.CompilerParams(
            collective_id=0, has_side_effects=True, vmem_limit_bytes=56522000
        ),
    )(*operands)


def solution(mesh):
    split = P(("pair", "row"), "col", None)
    return jax.shard_map(
        shards,
        mesh=mesh,
        in_specs=(split, split) + (P(),) * 8,
        out_specs=P(None, ("pair", "row"), "col"),
        check_vma=False,
    )
```
